256 devices in a mesh: blk: 16 (over x, y_lo, core), wide: 16 (over y_hi, z).
Axes of the slice: x: 4, y: 4 (y_hi: 2, y_lo: 2; y = y_hi * 2 + y_lo), z: 8, core: 2. Of those that a mesh axis runs over, the one named last changes fastest.
Arguments:
- points: bfloat16 [65536, 32], P(('blk', 'wide')), may hold values from -6 to 6
- inv_length: float32 [32], replicated, may hold values from 0.2 to 0.7
- noise_var: float32 [], replicated, may hold values from 0.1 to 1
- solution: float32 [65536, 128], P(('blk', 'wide')), may hold values from -6 to 6
- residual: float32 [65536, 128], P(('blk', 'wide')), may hold values from -6 to 6
- direction: float32 [65536, 128], P(('blk', 'wide')), may hold values from -6 to 6
Outputs:
- new_solution: float32 [65536, 128], P(('blk', 'wide'))
- new_residual: float32 [65536, 128], P(('blk', 'wide'))
- new_direction: float32 [65536, 128], P(('blk', 'wide'))
The draws below stay inside these ranges and needn't reach their ends.
All inputs are finite; a program needn't handle non-finite values.
Results may differ from the reference program's by a relative error of at most 0.01.
Values may be sent and summed in bfloat16 or wider, within the bound.
No kernel may reach another device: no remote copies, remote signals or barrier semaphores. Data moves between devices by JAX's collectives and lax.ppermute only.
A program may use at most 64 MiB of HBM per device.

```python
import math
import jax
import jax.numpy as jnp
from jax import lax

PIECE = 256
FEATURES = 32
RHS = 128
POINTS = 65536


def levels(rng, extent, shards, low, largest):
    def one(position, shards_of):
        steps = jax.random.uniform(jax.random.fold_in(jax.random.fold_in(rng, 6), position), (shards_of,), jnp.float32, low / len(shards), largest / len(shards))
        return jnp.repeat(jnp.exp(steps), extent[position] // shards_of).reshape((-1,) + (1,) * (len(extent) - position - 1))

    gain = one(*shards[0])
    for cut in shards[1:]:
        gain = gain * one(*cut)
    return gain


def noise(own_key, extent, spread, limit, cuts=(), kind=jnp.bfloat16):
    gain = levels(own_key, extent, cuts, -0.22, 0.18) if cuts else 1.0
    result = jax.random.normal(own_key, extent, jnp.float32) * spread * gain
    return jnp.minimum(jnp.maximum(result, -limit), limit).astype(kind)


def setup_inputs(seed: int = 0) -> dict:
    seeds = jax.random.split(jax.random.key(seed), 7)
    return {
        "points": noise(seeds[0], (POINTS, FEATURES), 1.0, 6.0, ((0, 256),)),
        "inv_length": jnp.clip(jnp.exp(jax.random.uniform(seeds[1], (FEATURES,), jnp.float32, math.log(0.2), math.log(0.7))), 0.2, 0.7),
        "noise_var": jnp.clip(jnp.exp(jax.random.uniform(seeds[2], (), jnp.float32, math.log(0.1), math.log(1.0))), 0.1, 1.0),
        "solution": noise(seeds[3], (POINTS, RHS), 1.0, 6.0, ((0, 256),), jnp.float32),
        "residual": noise(seeds[4], (POINTS, RHS), 1.0, 6.0, ((0, 256),), jnp.float32),
        "direction": noise(seeds[5], (POINTS, RHS), 1.0, 6.0, ((0, 256),), jnp.float32),
    }


def kernel_tile(rows_x, rows_sq, cols_x, cols_sq):
    inner_prod = jnp.dot(rows_x, cols_x.T, precision=lax.Precision.HIGHEST)
    dist_sq = jnp.maximum(rows_sq[:, None] + cols_sq[None, :] - 2.0 * inner_prod, 0.0)
    radius = jnp.sqrt(5.0 * dist_sq)
    rounded = ((1.0 + radius + radius * radius / 3.0) * jnp.exp(-radius)).astype(jnp.bfloat16)
    return lax.optimization_barrier(rounded).astype(jnp.float32)

def reference(points, inv_length, noise_var, solution, residual, direction):
    scaled = (points.astype(jnp.float32) * inv_length).astype(jnp.bfloat16)
    low_dir = direction.astype(jnp.bfloat16)
    wide_x = lax.optimization_barrier(scaled).astype(jnp.float32)
    wide_p = lax.optimization_barrier(low_dir).astype(jnp.float32)
    point_sq = lax.optimization_barrier(jnp.sum(wide_x * wide_x, axis=1))

    def row_block(block_index):
        start = (block_index * PIECE).astype(jnp.int32)
        rows_x = lax.dynamic_slice_in_dim(wide_x, start, PIECE, 0)
        rows_sq = lax.dynamic_slice_in_dim(point_sq, start, PIECE, 0)
        kernel_rows = kernel_tile(rows_x, rows_sq, wide_x, point_sq)
        return jnp.dot(kernel_rows, wide_p, precision=lax.Precision.HIGHEST)
    blocks = lax.map(row_block, jnp.arange(POINTS // PIECE, dtype=jnp.int32))
    kernel_image = blocks.reshape(POINTS, RHS) + noise_var * direction
    old_norm = lax.optimization_barrier(jnp.sum(residual * residual, axis=0))
    curvature = lax.optimization_barrier(jnp.sum(direction * kernel_image, axis=0))
    step_length = old_norm / curvature
    new_solution = solution + step_length * direction
    new_residual = residual - step_length * kernel_image
    new_norm = lax.optimization_barrier(jnp.sum(new_residual * new_residual, axis=0))
    new_direction = new_residual + new_norm / old_norm * direction
    return (new_solution, new_residual, new_direction)
```

```python
import functools
import math

import jax
import jax.numpy as jnp
from jax import lax
from jax.experimental import pallas as pl
from jax.experimental.pallas import tpu as pltpu
from jax.sharding import Mesh
from jax.sharding import PartitionSpec as P

AXES = ("x", "yl", "c", "yh", "z")
ROWS = ("x", "yl")
PLANE = ("x", "yl", "c", "yh")
FEATURES = 32
SCALE = 5.0 / 3.0
ROOT3 = math.sqrt(3.0)
LOG2E = 1.4426950408889634
VMEM = pltpu.CompilerParams(vmem_limit_bytes=48 * 2**20)


def split3(v):
    one = v.astype(jnp.bfloat16).astype(jnp.float32)
    rest = v - one
    two = rest.astype(jnp.bfloat16).astype(jnp.float32)
    return one, two, (rest - two)


def augmented(x4, quarter, is_row):
    k = lax.broadcasted_iota(jnp.int32, (128, 128), 0)
    l = lax.broadcasted_iota(jnp.int32, (128, 128), 1)
    mine = k // FEATURES == quarter
    spread = mine & (l < 96) & (k % FEATURES == l % FEATURES)
    total = mine & (l >= 96) & (l < 102)
    wide = x4.astype(jnp.float32)
    square = wide * wide
    high = square.astype(jnp.bfloat16)
    low = (square - high.astype(jnp.float32)).astype(jnp.bfloat16)
    to = lambda m: jnp.where(m, 1.0, 0.0).astype(jnp.bfloat16)
    dot = functools.partial(jnp.dot, preferred_element_type=jnp.float32)
    v = dot(x4, to(spread)) + dot(high, to(total)) + dot(low, to(total))
    lane = lax.broadcasted_iota(jnp.int32, (1, 128), 1)
    if is_row:
        one, two, three = split3(v * SCALE)
        tail = jnp.where(lane == 96, one, jnp.where(lane == 97, two, three))
        tail = jnp.where(lane < 99, tail, jnp.where(lane < 102, 1.0, 0.0))
        out = jnp.where(lane < 96, v, tail)
    else:
        one, two, three = split3(v * jnp.where(lane < 96, -2.0 * SCALE, SCALE))
        first = (lane < 32) | (lane == 99)
        second = ((lane >= 32) & (lane < 64)) | (lane == 100)
        out = jnp.where(first, one, jnp.where(second, two, three))
        out = jnp.where((lane >= 96) & (lane < 99), 1.0, out)
        out = jnp.where(lane < 102, out, 0.0)
    return out.astype(jnp.bfloat16)


def rows_kernel(x_ref, out_ref):
    n = x_ref.shape[0]
    x4 = x_ref[...].reshape(n * 64, 128)
    for q in range(4):
        out_ref[:, q * 64 : (q + 1) * 64, :] = augmented(x4, q, True).reshape(n, 64, 128)


def matern(u):
    m = jnp.maximum(u, 1e-30)
    t = m * lax.rsqrt(m)
    return (((1.0 + m) + ROOT3 * t) * jnp.exp2((-ROOT3 * LOG2E) * t)).astype(jnp.bfloat16)


def tiles_kernel(n_bundles, has_sum, last, row_tile, *refs):
    rows_ref, bundles, refs = refs[0], refs[1 : 1 + n_bundles], refs[1 + n_bundles :]
    if has_sum:
        sum_ref, refs = refs[0], refs[1:]
    out_ref, cols_ref, dirs_ref, acc_ref = refs
    pieces = bundles[0].shape[0]
    for b, bundle in enumerate(bundles):
        here = slice(b * pieces, (b + 1) * pieces)
        dirs_ref[here] = bundle[:, :256, :]
        x4 = bundle[:, 256:, :].reshape(pieces * 64, 128)
        for q in range(4):
            cols_ref[here, q * 64 : (q + 1) * 64, :] = augmented(x4, q, False).reshape(pieces, 64, 128)
    count = rows_ref.shape[0]

    def turn(n, first):
        for i in range(count // row_tile):
            at = slice(i * row_tile, (i + 1) * row_tile)
            u = lax.dot_general(
                rows_ref[at, :], cols_ref[n], (((1,), (1,)), ((), ())), preferred_element_type=jnp.float32
            )
            part = jnp.dot(matern(u), dirs_ref[n], preferred_element_type=jnp.float32)
            if first is None:
                acc_ref[at, :] = acc_ref[at, :] + part
            elif first:
                acc_ref[at, :] = part
            else:
                acc_ref[at, :] = sum_ref[at, :] + part

    turn(0, not has_sum)

    def body(n, _):
        turn(n, None)
        return 0

    lax.fori_loop(1, n_bundles * pieces, body, 0)
    out_ref[...] = acc_ref[...].astype(out_ref.dtype)


def tiles(rows, bundles, so_far, last):
    pieces = bundles[0].shape[0]
    n = len(bundles) * pieces
    count = rows.shape[0]
    args = (rows, *bundles) + (() if so_far is None else (so_far,))
    whole = pl.BlockSpec(memory_space=pltpu.VMEM)
    return pl.pallas_call(
        functools.partial(tiles_kernel, len(bundles), so_far is not None, last, min(count, 1024)),
        out_shape=jax.ShapeDtypeStruct((count, 128), jnp.bfloat16 if last else jnp.float32),
        in_specs=[whole] * len(args),
        out_specs=whole,
        scratch_shapes=[
            pltpu.VMEM((n, 256, 128), jnp.bfloat16),
            pltpu.VMEM((n, 256, 128), jnp.bfloat16),
            pltpu.VMEM((count, 128), jnp.float32),
        ],
        compiler_params=VMEM,
        cost_estimate=pl.CostEstimate(
            flops=2 * count * n * 256 * 256 * 2, bytes_accessed=2 * count * 128 * 4, transcendentals=count * n * 512
        ),
    )(*args)


def image_kernel(parts_ref, noise_ref, dir_ref, res_ref, image_ref, sums_ref):
    image = jnp.sum(parts_ref[...].astype(jnp.float32), axis=0) + noise_ref[0, 0] * dir_ref[...]
    image_ref[...] = image
    res = res_ref[...]
    col = lambda v: jnp.sum(v, axis=0, keepdims=True)
    sums_ref[0:1, :] = col(res * res)
    sums_ref[1:2, :] = col(dir_ref[...] * image)
    sums_ref[2:3, :] = col(res * image)
    sums_ref[3:4, :] = col(image * image)
    sums_ref[4:8, :] = jnp.zeros((4, 128), jnp.float32)


def step_kernel(sums_ref, image_ref, sol_ref, res_ref, dir_ref, new_sol, new_res, new_dir):
    sums = jnp.sum(sums_ref[...], axis=0)
    old_norm, curvature, cross, image_sq = (sums[i : i + 1, :] for i in range(4))
    step = old_norm / curvature
    new_norm = jnp.maximum(old_norm - 2.0 * step * cross + step * step * image_sq, 0.0)
    direction = dir_ref[...]
    new_sol[...] = sol_ref[...] + step * direction
    residual = res_ref[...] - step * image_ref[...]
    new_res[...] = residual
    new_dir[...] = residual + (new_norm / old_norm) * direction


def turned(x, axis, by):
    count = lax.axis_size(axis)
    return lax.ppermute(x, axis, [(i, (i + by) % count) for i in range(count)])


def from_all(x, axes):
    count = lax.axis_size(axes)
    return lax.all_to_all(jnp.broadcast_to(x[None], (count,) + x.shape), axes, 0, 0, tiled=True)


def on_device(points, inv_length, noise_var, solution, residual, direction):
    scaled = (points.astype(jnp.float32) * inv_length).astype(jnp.bfloat16)
    x4 = jnp.concatenate([scaled[q * 64 : (q + 1) * 64] for q in range(4)], axis=1)
    packed = jnp.concatenate([direction.astype(jnp.bfloat16), x4], axis=0)[None]
    pair = jnp.concatenate([packed, turned(packed, "yh", 1)], axis=0)
    whole = pl.BlockSpec(memory_space=pltpu.VMEM)

    n_rows = lax.axis_size(ROWS)
    rows = pl.pallas_call(
        rows_kernel,
        out_shape=jax.ShapeDtypeStruct((n_rows, 256, 128), jnp.bfloat16),
        in_specs=[whole],
        out_specs=whole,
        compiler_params=VMEM,
    )(from_all(x4, ROWS)).reshape(n_rows * 256, 128)

    length = lax.axis_size("z")
    up = down = pair
    so_far = None
    here = [pair]
    for hop in range(length // 2 + 1):
        bundles = [b for h in here for b in (h, turned(h, "c", 1))]
        if hop < length // 2 - 1:
            up, down = turned(up, "z", 1), turned(down, "z", -1)
            here = [up, down]
        else:
            up = turned(up, "z", 1)
            here = [up]
        so_far = tiles(rows, bundles, so_far, hop == length // 2)
    parts = lax.all_to_all(so_far.reshape(n_rows, 256, 128), ROWS, 0, 0, tiled=True)
    f32 = jax.ShapeDtypeStruct(direction.shape, jnp.float32)
    image, sums = pl.pallas_call(
        image_kernel,
        out_shape=(f32, jax.ShapeDtypeStruct((8, 128), jnp.float32)),
        in_specs=[whole, pl.BlockSpec(memory_space=pltpu.SMEM), whole, whole],
        out_specs=(whole, whole),
        compiler_params=VMEM,
    )(parts, noise_var.reshape(1, 1), direction, residual)
    sums = jnp.sum(from_all(sums, PLANE), axis=0)
    sums = from_all(sums, ("z",))
    return pl.pallas_call(
        step_kernel,
        out_shape=(f32, f32, f32),
        in_specs=[whole] * 5,
        out_specs=(whole,) * 3,
        compiler_params=VMEM,
    )(sums, image, solution, residual, direction)


def solution(mesh):
    finer = Mesh(mesh.devices.reshape(4, 2, 2, 2, 8), AXES)
    placed = P(AXES, None)
    return jax.shard_map(
        on_device,
        mesh=finer,
        in_specs=(placed, P(), P(), placed, placed, placed),
        out_specs=(placed,) * 3,
        check_vma=False,
    )
```

```python
import functools
import math

import jax
import jax.numpy as jnp
from jax import lax
from jax.experimental import pallas as pl
from jax.experimental.pallas import tpu as pltpu
from jax.sharding import Mesh
from jax.sharding import PartitionSpec as P

AXES = ("x", "yl", "c", "yh", "z")
ROWS = ("x", "yl")
PLANE = ("x", "yl", "c", "yh")
FEATURES = 32
SCALE = 5.0 / 3.0
ROOT3 = math.sqrt(3.0)
LOG2E = 1.4426950408889634
VMEM = pltpu.CompilerParams(vmem_limit_bytes=48 * 2**20)


def split3(v):
    one = v.astype(jnp.bfloat16).astype(jnp.float32)
    rest = v - one
    two = rest.astype(jnp.bfloat16).astype(jnp.float32)
    return one, two, (rest - two)


def augmented(x4, quarter, is_row):
    k = lax.broadcasted_iota(jnp.int32, (128, 128), 0)
    l = lax.broadcasted_iota(jnp.int32, (128, 128), 1)
    mine = k // FEATURES == quarter
    spread = mine & (l < 96) & (k % FEATURES == l % FEATURES)
    total = mine & (l >= 96) & (l < 102)
    wide = x4.astype(jnp.float32)
    square = wide * wide
    high = square.astype(jnp.bfloat16)
    low = (square - high.astype(jnp.float32)).astype(jnp.bfloat16)
    to = lambda m: jnp.where(m, 1.0, 0.0).astype(jnp.bfloat16)
    dot = functools.partial(jnp.dot, preferred_element_type=jnp.float32)
    v = dot(x4, to(spread)) + dot(high, to(total)) + dot(low, to(total))
    lane = lax.broadcasted_iota(jnp.int32, (1, 128), 1)
    if is_row:
        one, two, three = split3(v * SCALE)
        tail = jnp.where(lane == 96, one, jnp.where(lane == 97, two, three))
        tail = jnp.where(lane < 99, tail, jnp.where(lane < 102, 1.0, 0.0))
        out = jnp.where(lane < 96, v, tail)
    else:
        one, two, three = split3(v * jnp.where(lane < 96, -2.0 * SCALE, SCALE))
        first = (lane < 32) | (lane == 99)
        second = ((lane >= 32) & (lane < 64)) | (lane == 100)
        out = jnp.where(first, one, jnp.where(second, two, three))
        out = jnp.where((lane >= 96) & (lane < 99), 1.0, out)
        out = jnp.where(lane < 102, out, 0.0)
    return out.astype(jnp.bfloat16)


def rows_kernel(x_ref, out_ref):
    n = x_ref.shape[0]
    x4 = x_ref[...].reshape(n * 64, 128)
    for q in range(4):
        out_ref[:, q * 64 : (q + 1) * 64, :] = augmented(x4, q, True).reshape(n, 64, 128)


def matern(u):
    m = jnp.maximum(u, 1e-30)
    t = m * lax.rsqrt(m)
    return (((1.0 + m) + ROOT3 * t) * jnp.exp2((-ROOT3 * LOG2E) * t)).astype(jnp.bfloat16)


def tiles_kernel(n_bundles, has_sum, *refs):
    rows_ref, bundles, refs = refs[0], refs[1 : 1 + n_bundles], refs[1 + n_bundles :]
    if has_sum:
        sum_ref, refs = refs[0], refs[1:]
    out_ref, cols_ref, acc_ref, ahead_ref = refs
    pieces = bundles[0].shape[0]
    total = n_bundles * pieces
    for b, bundle in enumerate(bundles):
        x4 = bundle[:, 256:, :].reshape(pieces * 64, 128)
        for q in range(4):
            cols_ref[b * pieces : (b + 1) * pieces, q * 64 : (q + 1) * 64, :] = augmented(x4, q, False).reshape(
                pieces, 64, 128
            )

    def distances(n):
        ahead_ref[n % 2] = lax.dot_general(
            rows_ref[...], cols_ref[n], (((1,), (1,)), ((), ())), preferred_element_type=jnp.float32
        )

    distances(0)
    for n in range(total):
        if n + 1 < total:
            distances(n + 1)
        part = jnp.dot(
            matern(ahead_ref[n % 2]), bundles[n // pieces][n % pieces, :256, :], preferred_element_type=jnp.float32
        )
        if n > 0:
            part = acc_ref[...] + part
        elif has_sum:
            part = sum_ref[...] + part
        if n + 1 < total:
            acc_ref[...] = part
        else:
            out_ref[...] = part.astype(out_ref.dtype)


def tiles(rows, bundles, so_far, last=False):
    pieces = bundles[0].shape[0]
    n = len(bundles) * pieces
    count = rows.shape[0]
    args = (rows, *bundles) + (() if so_far is None else (so_far,))
    whole = pl.BlockSpec(memory_space=pltpu.VMEM)
    return pl.pallas_call(
        functools.partial(tiles_kernel, len(bundles), so_far is not None),
        out_shape=jax.ShapeDtypeStruct((count, 128), jnp.bfloat16 if last else jnp.float32),
        in_specs=[whole] * len(args),
        out_specs=whole,
        scratch_shapes=[
            pltpu.VMEM((n, 256, 128), jnp.bfloat16),
            pltpu.VMEM((count, 128), jnp.float32),
            pltpu.VMEM((2, count, 256), jnp.float32),
        ],
        compiler_params=VMEM,
        cost_estimate=pl.CostEstimate(
            flops=2 * count * n * 256 * 256 * 2 // 4, bytes_accessed=0, transcendentals=0
        ),
    )(*args)


def image_kernel(parts_ref, noise_ref, dir_ref, res_ref, image_ref, sums_ref):
    image = jnp.sum(parts_ref[...].astype(jnp.float32), axis=0) + noise_ref[0, 0] * dir_ref[...]
    image_ref[...] = image
    res = res_ref[...]
    col = lambda v: jnp.sum(v, axis=0, keepdims=True)
    sums_ref[0:1, :] = col(res * res)
    sums_ref[1:2, :] = col(dir_ref[...] * image)
    sums_ref[2:3, :] = col(res * image)
    sums_ref[3:4, :] = col(image * image)


def step_kernel(sums_ref, image_ref, sol_ref, res_ref, dir_ref, new_sol, new_res, new_dir):
    sums = jnp.sum(sums_ref[...], axis=0)
    old_norm, curvature, cross, image_sq = (sums[i : i + 1, :] for i in range(4))
    step = old_norm / curvature
    new_norm = jnp.maximum(old_norm - 2.0 * step * cross + step * step * image_sq, 0.0)
    direction = dir_ref[...]
    new_sol[...] = sol_ref[...] + step * direction
    residual = res_ref[...] - step * image_ref[...]
    new_res[...] = residual
    new_dir[...] = residual + (new_norm / old_norm) * direction


def turned(x, axis, by):
    count = lax.axis_size(axis)
    return lax.ppermute(x, axis, [(i, (i + by) % count) for i in range(count)])


def from_all(x, axes):
    count = lax.axis_size(axes)
    return lax.all_to_all(jnp.broadcast_to(x[None], (count,) + x.shape), axes, 0, 0, tiled=True)


def on_device(points, inv_length, noise_var, solution, residual, direction):
    scaled = (points.astype(jnp.float32) * inv_length).astype(jnp.bfloat16)
    x4 = jnp.concatenate([scaled[q * 64 : (q + 1) * 64] for q in range(4)], axis=1)
    packed = jnp.concatenate([direction.astype(jnp.bfloat16), x4], axis=0)[None]
    pair = jnp.concatenate([packed, turned(packed, "yh", 1)], axis=0)
    whole = pl.BlockSpec(memory_space=pltpu.VMEM)

    n_rows = lax.axis_size(ROWS)
    rows = pl.pallas_call(
        rows_kernel,
        out_shape=jax.ShapeDtypeStruct((n_rows, 256, 128), jnp.bfloat16),
        in_specs=[whole],
        out_specs=whole,
        compiler_params=VMEM,
    )(from_all(x4, ROWS)).reshape(n_rows * 256, 128)

    def after(x, done):
        return lax.optimization_barrier((x, done))[0]

    length = lax.axis_size("z")
    ring = [pair, turned(pair, "z", 1), turned(after(pair, rows), "z", -1)]
    so_far = tiles(rows, [pair, turned(pair, "c", 1)], None)
    others = None
    for slot in range(1, length):
        if slot + 2 < length:
            ring.append(turned(after(ring[slot], so_far), "z", 1 if slot % 2 else -1))
        bundle = ring[slot]
        mine = [bundle]
        other = turned(after(bundle, so_far) if slot > 1 else bundle, "c", 1)
        if slot == 1:
            mine.append(other)
            other = None
        if others is not None:
            mine.insert(0, others)
        so_far = tiles(rows, mine, so_far)
        others = other
    so_far = tiles(rows, [others], so_far, True)
    parts = lax.all_to_all(so_far.reshape(n_rows, 256, 128), ROWS, 0, 0, tiled=True)
    f32 = jax.ShapeDtypeStruct(direction.shape, jnp.float32)
    image, sums = pl.pallas_call(
        image_kernel,
        out_shape=(f32, jax.ShapeDtypeStruct((4, 128), jnp.float32)),
        in_specs=[whole, pl.BlockSpec(memory_space=pltpu.SMEM), whole, whole],
        out_specs=(whole, whole),
        compiler_params=VMEM,
    )(parts, noise_var.reshape(1, 1), direction, residual)
    sums = jnp.sum(from_all(sums, PLANE), axis=0)
    sums = from_all(sums, ("z",))
    return pl.pallas_call(
        step_kernel,
        out_shape=(f32, f32, f32),
        in_specs=[whole] * 5,
        out_specs=(whole,) * 3,
        compiler_params=VMEM,
    )(sums, image, solution, residual, direction)


def solution(mesh):
    finer = Mesh(mesh.devices.reshape(4, 2, 2, 2, 8), AXES)
    placed = P(AXES, None)
    return jax.shard_map(
        on_device,
        mesh=finer,
        in_specs=(placed, P(), P(), placed, placed, placed),
        out_specs=(placed,) * 3,
        check_vma=False,
    )
```

```python
import functools
import math

import jax
import jax.numpy as jnp
from jax import lax
from jax.experimental import pallas as pl
from jax.experimental.pallas import tpu as pltpu
from jax.sharding import Mesh
from jax.sharding import PartitionSpec as P

AXES = ("xh", "xl", "yl", "c", "yh", "zh", "zm", "zl")
ROWS = ("xh", "yh", "zm")
CUBE = ("xl", "yl", "zl")
PLANE = ("xh", "xl", "yl", "c", "yh")
DEPTH = ("zh", "zm", "zl")
FEATURES = 32
SCALE = 5.0 / 3.0
ROOT3 = math.sqrt(3.0)
LOG2E = 1.4426950408889634
VMEM = pltpu.CompilerParams(vmem_limit_bytes=48 * 2**20)


def split3(v):
    one = v.astype(jnp.bfloat16).astype(jnp.float32)
    rest = v - one
    two = rest.astype(jnp.bfloat16).astype(jnp.float32)
    return one, two, (rest - two)


def augmented(x4, quarter, is_row):
    k = lax.broadcasted_iota(jnp.int32, (128, 128), 0)
    l = lax.broadcasted_iota(jnp.int32, (128, 128), 1)
    mine = k // FEATURES == quarter
    spread = mine & (l < 96) & (k % FEATURES == l % FEATURES)
    total = mine & (l >= 96) & (l < 102)
    wide = x4.astype(jnp.float32)
    square = wide * wide
    high = square.astype(jnp.bfloat16)
    low = (square - high.astype(jnp.float32)).astype(jnp.bfloat16)
    to = lambda m: jnp.where(m, 1.0, 0.0).astype(jnp.bfloat16)
    dot = functools.partial(jnp.dot, preferred_element_type=jnp.float32)
    v = dot(x4, to(spread)) + dot(high, to(total)) + dot(low, to(total))
    lane = lax.broadcasted_iota(jnp.int32, (1, 128), 1)
    if is_row:
        one, two, three = split3(v * SCALE)
        tail = jnp.where(lane == 96, one, jnp.where(lane == 97, two, three))
        tail = jnp.where(lane < 99, tail, jnp.where(lane < 102, 1.0, 0.0))
        out = jnp.where(lane < 96, v, tail)
    else:
        one, two, three = split3(v * jnp.where(lane < 96, -2.0 * SCALE, SCALE))
        first = (lane < 32) | (lane == 99)
        second = ((lane >= 32) & (lane < 64)) | (lane == 100)
        out = jnp.where(first, one, jnp.where(second, two, three))
        out = jnp.where((lane >= 96) & (lane < 99), 1.0, out)
        out = jnp.where(lane < 102, out, 0.0)
    return out.astype(jnp.bfloat16)


def rows_kernel(x_ref, out_ref):
    n = x_ref.shape[0]
    x4 = x_ref[...].reshape(n * 64, 128)
    for q in range(4):
        out_ref[:, q * 64 : (q + 1) * 64, :] = augmented(x4, q, True).reshape(n, 64, 128)


def matern(u):
    m = jnp.maximum(u, 1e-30)
    t = m * lax.rsqrt(m)
    return (((1.0 + m) + ROOT3 * t) * jnp.exp2((-ROOT3 * LOG2E) * t)).astype(jnp.bfloat16)


def tiles_kernel(n_bundles, has_sum, tile, unroll, *refs):
    rows_ref, bundles, refs = refs[0], refs[1 : 1 + n_bundles], refs[1 + n_bundles :]
    if has_sum:
        sum_ref, refs = refs[0], refs[1:]
    out_ref, cols_ref, dirs_ref, acc_ref, ahead_ref = refs
    pieces = bundles[0].shape[0]
    for b, bundle in enumerate(bundles):
        here = slice(b * pieces, (b + 1) * pieces)
        dirs_ref[here] = bundle[:, :256, :]

        def quarter(q, _):
            x4 = bundle[:, 256:, :].reshape(pieces * 64, 128)
            cols_ref[here, pl.ds(pl.multiple_of(q * 64, 64), 64), :] = augmented(x4, q, False).reshape(pieces, 64, 128)
            return 0

        lax.fori_loop(0, 4, quarter, 0)
    per_piece = rows_ref.shape[0] // tile
    total = n_bundles * pieces * per_piece
    acc_ref[...] = sum_ref[...] if has_sum else jnp.zeros_like(acc_ref)

    def at(k):
        return pl.ds(pl.multiple_of((k % per_piece) * tile, tile), tile)

    def distances(k, slot):
        ahead_ref[slot] = lax.dot_general(
            rows_ref[at(k), :], cols_ref[k // per_piece], (((1,), (1,)), ((), ())), preferred_element_type=jnp.float32
        )

    distances(0, 0)

    def body(turn, _):
        for s in range(unroll):
            k = turn * unroll + s
            distances(jnp.minimum(k + 1, total - 1), (s + 1) % 2)
            acc_ref[at(k), :] += jnp.dot(
                matern(ahead_ref[s % 2]), dirs_ref[k // per_piece], preferred_element_type=jnp.float32
            )
        return 0

    lax.fori_loop(0, total // unroll, body, 0)
    out_ref[...] = acc_ref[...].astype(out_ref.dtype)


def tiles(rows, bundles, so_far, last=False):
    pieces = bundles[0].shape[0]
    n = len(bundles) * pieces
    count = rows.shape[0]
    tile = 1024
    args = (rows, *bundles) + (() if so_far is None else (so_far,))
    whole = pl.BlockSpec(memory_space=pltpu.VMEM)
    return pl.pallas_call(
        functools.partial(tiles_kernel, len(bundles), so_far is not None, tile, 2),
        out_shape=jax.ShapeDtypeStruct((count, 128), jnp.bfloat16 if last else jnp.float32),
        in_specs=[whole] * len(args),
        out_specs=whole,
        scratch_shapes=[
            pltpu.VMEM((n, 256, 128), jnp.bfloat16),
            pltpu.VMEM((n, 256, 128), jnp.bfloat16),
            pltpu.VMEM((count, 128), jnp.float32),
            pltpu.VMEM((2, tile, 256), jnp.float32),
        ],
        compiler_params=VMEM,
        cost_estimate=pl.CostEstimate(
            flops=count * n * 256 * 256, bytes_accessed=0, transcendentals=0
        ),
    )(*args)


def image_kernel(parts_ref, noise_ref, dir_ref, res_ref, image_ref, sums_ref):
    image = jnp.sum(parts_ref[...].astype(jnp.float32), axis=0) + noise_ref[0, 0] * dir_ref[...]
    image_ref[...] = image
    res = res_ref[...]
    col = lambda v: jnp.sum(v, axis=0, keepdims=True)
    sums_ref[0:1, :] = col(res * res)
    sums_ref[1:2, :] = col(dir_ref[...] * image)
    sums_ref[2:3, :] = col(res * image)
    sums_ref[3:4, :] = col(image * image)


def step_kernel(sums_ref, image_ref, sol_ref, res_ref, dir_ref, new_sol, new_res, new_dir):
    sums = jnp.sum(sums_ref[...], axis=0)
    old_norm, curvature, cross, image_sq = (sums[i : i + 1, :] for i in range(4))
    step = old_norm / curvature
    new_norm = jnp.maximum(old_norm - 2.0 * step * cross + step * step * image_sq, 0.0)
    direction = dir_ref[...]
    new_sol[...] = sol_ref[...] + step * direction
    residual = res_ref[...] - step * image_ref[...]
    new_res[...] = residual
    new_dir[...] = residual + (new_norm / old_norm) * direction


def turned(x, axis, by):
    count = lax.axis_size(axis)
    return lax.ppermute(x, axis, [(i, (i + by) % count) for i in range(count)])


def mirrored(x, axes):
    count = lax.axis_size(axes)
    return lax.ppermute(x, axes, [(i, count - 1 - i) for i in range(count)])


def from_all(x, axes):
    count = lax.axis_size(axes)
    return lax.all_to_all(jnp.broadcast_to(x[None], (count,) + x.shape), axes, 0, 0, tiled=True)


def on_device(points, inv_length, noise_var, solution, residual, direction):
    scaled = (points.astype(jnp.float32) * inv_length).astype(jnp.bfloat16)
    x4 = jnp.concatenate([scaled[q * 64 : (q + 1) * 64] for q in range(4)], axis=1)
    packed = jnp.concatenate([direction.astype(jnp.bfloat16), x4], axis=0)[None]
    pair = jnp.concatenate([packed, mirrored(packed, DEPTH)], axis=0)
    whole = pl.BlockSpec(memory_space=pltpu.VMEM)

    n_rows = lax.axis_size(ROWS)
    rows = pl.pallas_call(
        rows_kernel,
        out_shape=jax.ShapeDtypeStruct((n_rows, 256, 128), jnp.bfloat16),
        in_specs=[whole],
        out_specs=whole,
        compiler_params=VMEM,
    )(from_all(x4, ROWS)).reshape(n_rows * 256, 128)

    def after(x, done):
        return lax.optimization_barrier((x, done))[0]

    own = after(pair, rows)
    near = [turned(own, a, 1) for a in CUBE]
    so_far = tiles(rows, [own, turned(own, "c", 1)], None)
    near = after(near, so_far)
    other = [turned(b, "c", 1) for b in near]
    far = [turned(near[(i + 1) % 3], a, 1) for i, a in enumerate(CUBE)]
    so_far = tiles(rows, near, so_far)
    so_far = tiles(rows, other, so_far)
    far = after(far, so_far)
    opposite = turned(far[0], CUBE[2], 1)
    other = [turned(b, "c", 1) for b in far]
    so_far = tiles(rows, far, so_far)
    opposite = after(opposite, so_far)
    opposite = [opposite, turned(opposite, "c", 1)]
    so_far = tiles(rows, other, so_far)
    so_far = tiles(rows, opposite, so_far, True)
    parts = lax.all_to_all(so_far.reshape(n_rows, 256, 128), ROWS, 0, 0, tiled=True)
    f32 = jax.ShapeDtypeStruct(direction.shape, jnp.float32)
    image, sums = pl.pallas_call(
        image_kernel,
        out_shape=(f32, jax.ShapeDtypeStruct((4, 128), jnp.float32)),
        in_specs=[whole, pl.BlockSpec(memory_space=pltpu.SMEM), whole, whole],
        out_specs=(whole, whole),
        compiler_params=VMEM,
    )(parts, noise_var.reshape(1, 1), direction, residual)
    sums = jnp.sum(from_all(sums, PLANE), axis=0)
    sums = from_all(sums, DEPTH)
    return pl.pallas_call(
        step_kernel,
        out_shape=(f32, f32, f32),
        in_specs=[whole] * 5,
        out_specs=(whole,) * 3,
        compiler_params=VMEM,
    )(sums, image, solution, residual, direction)


def solution(mesh):
    finer = Mesh(mesh.devices.reshape((2,) * 8), AXES)
    placed = P(AXES, None)
    return jax.shard_map(
        on_device,
        mesh=finer,
        in_specs=(placed, P(), P(), placed, placed, placed),
        out_specs=(placed,) * 3,
        check_vma=False,
    )
```

```python
import functools
import math

import jax
import jax.numpy as jnp
from jax import lax
from jax.experimental import pallas as pl
from jax.experimental.pallas import tpu as pltpu
from jax.sharding import Mesh
from jax.sharding import PartitionSpec as P

AXES = ("xh", "xl", "yl", "c", "yh", "zh", "zm", "zl")
ROWS = ("xh", "xl", "yl")
NEAR = ("zl", "yh", "zm")
PLANE = ("xh", "xl", "yl", "c", "yh")
DEPTH = ("zh", "zm", "zl")
FEATURES = 32
LOG2E = 1.4426950408889634
VMEM = pltpu.CompilerParams(vmem_limit_bytes=48 * 2**20)


def split3(v):
    one = v.astype(jnp.bfloat16).astype(jnp.float32)
    rest = v - one
    two = rest.astype(jnp.bfloat16).astype(jnp.float32)
    return one, two, rest - two


def prep_kernel(points_ref, inv_ref, dir_ref, row_ref, packed_ref):
    count = points_ref.shape[1]
    square = (FEATURES, FEATURES)
    diagonal = lax.broadcasted_iota(jnp.int32, square, 0) == lax.broadcasted_iota(jnp.int32, square, 1)
    inverse = jnp.sum(jnp.where(diagonal, inv_ref[...], 0.0), axis=1, keepdims=True)
    x = (points_ref[...].astype(jnp.float32) * inverse).astype(jnp.bfloat16).astype(jnp.float32)
    parts = split3(jnp.sum(x * x, axis=0, keepdims=True))
    place = lax.broadcasted_iota(jnp.int32, (FEATURES, count), 0)

    def operand(front, squares_at, ones_at):
        tail = jnp.where((place >= ones_at) & (place < ones_at + 3), 1.0, 0.0)
        for i, part in enumerate(parts):
            tail = jnp.where(place == squares_at + i, part, tail)
        half = count // 2
        stacked = jnp.concatenate([front[:, :half], tail[:, :half], front[:, half:], tail[:, half:]], axis=0)
        return stacked.T.astype(jnp.bfloat16)

    row_ref[...] = operand(x, 0, 3)
    packed_ref[0, :256, :] = dir_ref[...].astype(jnp.bfloat16)
    packed_ref[0, 256:, :] = operand(-2.0 * x, 3, 0)


def rows_kernel(x_ref, out_ref):
    lane = lax.broadcasted_iota(jnp.int32, (1, 128), 1)
    for j in range(x_ref.shape[0]):
        v = x_ref[j].astype(jnp.float32)
        r = pltpu.roll(v, 64, 1)
        out_ref[j, :128, :] = jnp.where(lane < 64, v, r).astype(jnp.bfloat16)
        out_ref[j, 128:, :] = jnp.where(lane < 64, r, v).astype(jnp.bfloat16)


def matern(d):
    m = jnp.maximum(d, 1e-30)
    t = m * lax.rsqrt(m)
    return (((m + 0.6) + (3.0 / math.sqrt(5.0)) * t) * jnp.exp2((-math.sqrt(5.0) * LOG2E) * t)).astype(jnp.bfloat16)


def tiles_kernel(n_bundles, has_sum, *refs):
    rows_ref, bundles, refs = refs[0], refs[1 : 1 + n_bundles], refs[1 + n_bundles :]
    if has_sum:
        sum_ref, refs = refs[0], refs[1:]
    out_ref, cols_ref, dirs_ref, acc_ref, ahead_ref = refs
    pieces = bundles[0].shape[0]
    total = n_bundles * pieces
    lane = lax.broadcasted_iota(jnp.int32, (1, 128), 1)
    first = jnp.where(lane < 64, 1.0, 0.0).astype(jnp.bfloat16)
    second = jnp.where(lane < 64, 0.0, 1.0).astype(jnp.bfloat16)
    for n in range(total):
        bundle = bundles[n // pieces]
        dirs_ref[n] = bundle[n % pieces, :256, :]
        both = bundle[n % pieces, 256:, :]
        cols_ref[n, :128, :] = both * first
        cols_ref[n, 128:, :] = both * second
    acc_ref[...] = sum_ref[...] if has_sum else jnp.zeros_like(acc_ref)

    def distances(n, slot):
        ahead_ref[slot] = lax.dot_general(
            rows_ref[...], cols_ref[n], (((1,), (1,)), ((), ())), preferred_element_type=jnp.float32
        )

    distances(0, 0)

    def body(turn, _):
        for s in range(2):
            n = turn * 2 + s
            distances(jnp.minimum(n + 1, total - 1), 1 - s)
            acc_ref[...] += jnp.dot(matern(ahead_ref[s]), dirs_ref[n], preferred_element_type=jnp.float32)
        return 0

    lax.fori_loop(0, total // 2, body, 0)
    out_ref[...] = acc_ref[...].astype(out_ref.dtype)


def tiles(rows, bundles, so_far, last=False):
    pieces = bundles[0].shape[0]
    n = len(bundles) * pieces
    count = rows.shape[0]
    args = (rows, *bundles) + (() if so_far is None else (so_far,))
    whole = pl.BlockSpec(memory_space=pltpu.VMEM)
    return pl.pallas_call(
        functools.partial(tiles_kernel, len(bundles), so_far is not None),
        out_shape=jax.ShapeDtypeStruct((count, 128), jnp.bfloat16 if last else jnp.float32),
        in_specs=[whole] * len(args),
        out_specs=whole,
        scratch_shapes=[
            pltpu.VMEM((n, 256, 128), jnp.bfloat16),
            pltpu.VMEM((n, 256, 128), jnp.bfloat16),
            pltpu.VMEM((count, 128), jnp.float32),
            pltpu.VMEM((2, count, 256), jnp.float32),
        ],
        compiler_params=VMEM,
        cost_estimate=pl.CostEstimate(flops=count * n * 256 * 256, bytes_accessed=0, transcendentals=0),
    )(*args)


def image_kernel(parts_ref, noise_ref, dir_ref, res_ref, image_ref, sums_ref):
    image = (5.0 / 3.0) * jnp.sum(parts_ref[...].astype(jnp.float32), axis=0) + noise_ref[0, 0] * dir_ref[...]
    image_ref[...] = image
    res = res_ref[...]
    col = lambda v: jnp.sum(v, axis=0, keepdims=True)
    sums_ref[0:1, :] = col(res * res)
    sums_ref[1:2, :] = col(dir_ref[...] * image)
    sums_ref[2:3, :] = col(res * image)
    sums_ref[3:4, :] = col(image * image)


def step_kernel(sums_ref, image_ref, sol_ref, res_ref, dir_ref, new_sol, new_res, new_dir):
    sums = jnp.sum(sums_ref[...], axis=0)
    old_norm, curvature, cross, image_sq = (sums[i : i + 1, :] for i in range(4))
    step = old_norm / curvature
    new_norm = jnp.maximum(old_norm - 2.0 * step * cross + step * step * image_sq, 0.0)
    direction = dir_ref[...]
    new_sol[...] = sol_ref[...] + step * direction
    residual = res_ref[...] - step * image_ref[...]
    new_res[...] = residual
    new_dir[...] = residual + (new_norm / old_norm) * direction


def turned(x, axis, by):
    count = lax.axis_size(axis)
    return lax.ppermute(x, axis, [(i, (i + by) % count) for i in range(count)])


def mirrored(x, axes):
    count = lax.axis_size(axes)
    return lax.ppermute(x, axes, [(i, count - 1 - i) for i in range(count)])


def from_all(x, axes):
    count = lax.axis_size(axes)
    return lax.all_to_all(jnp.broadcast_to(x[None], (count,) + x.shape), axes, 0, 0, tiled=True)


def on_device(points, inv_length, noise_var, solution, residual, direction):
    whole = pl.BlockSpec(memory_space=pltpu.VMEM)

    def after(x, done):
        return lax.optimization_barrier((x, done))[0]

    row, packed = pl.pallas_call(
        prep_kernel,
        out_shape=(
            jax.ShapeDtypeStruct((128, 128), jnp.bfloat16),
            jax.ShapeDtypeStruct((1, 384, 128), jnp.bfloat16),
        ),
        in_specs=[whole] * 3,
        out_specs=(whole,) * 2,
        compiler_params=VMEM,
    )(points.T, inv_length.reshape(1, FEATURES), direction)

    mirror = mirrored(packed, DEPTH)
    n_rows = lax.axis_size(ROWS)
    rows = pl.pallas_call(
        rows_kernel,
        out_shape=jax.ShapeDtypeStruct((n_rows, 256, 128), jnp.bfloat16),
        in_specs=[whole],
        out_specs=whole,
        compiler_params=VMEM,
    )(from_all(row, ROWS)).reshape(n_rows * 256, 128)
    pair = jnp.concatenate([packed, mirror], axis=0)
    own = after(pair, rows)
    near = [turned(own, a, 1) for a in NEAR]
    so_far = tiles(rows, [own, turned(own, "c", 1)], None)
    near = after(near, so_far)
    other = [turned(b, "c", 1) for b in near]
    far = [turned(near[(i + 1) % 3], a, 1) for i, a in enumerate(NEAR)]
    so_far = tiles(rows, near, so_far)
    so_far = tiles(rows, other, so_far)
    far = after(far, so_far)
    opposite = turned(far[0], NEAR[2], 1)
    other = [turned(b, "c", 1) for b in far]
    so_far = tiles(rows, far, so_far)
    opposite = after(opposite, so_far)
    opposite = [opposite, turned(opposite, "c", 1)]
    so_far = tiles(rows, other, so_far)
    so_far = tiles(rows, opposite, so_far, True)
    parts = lax.all_to_all(so_far.reshape(n_rows, 256, 128), ROWS, 0, 0, tiled=True)
    f32 = jax.ShapeDtypeStruct(direction.shape, jnp.float32)
    image, sums = pl.pallas_call(
        image_kernel,
        out_shape=(f32, jax.ShapeDtypeStruct((4, 128), jnp.float32)),
        in_specs=[whole, pl.BlockSpec(memory_space=pltpu.SMEM), whole, whole],
        out_specs=(whole, whole),
        compiler_params=VMEM,
    )(parts, noise_var.reshape(1, 1), direction, residual)
    sums = jnp.sum(from_all(sums, PLANE), axis=0)
    sums = from_all(sums, DEPTH)
    return pl.pallas_call(
        step_kernel,
        out_shape=(f32, f32, f32),
        in_specs=[whole] * 5,
        out_specs=(whole,) * 3,
        compiler_params=VMEM,
    )(sums, image, solution, residual, direction)


def solution(mesh):
    finer = Mesh(mesh.devices.reshape((2,) * 8), AXES)
    placed = P(AXES, None)
    return jax.shard_map(
        on_device,
        mesh=finer,
        in_specs=(placed, P(), P(), placed, placed, placed),
        out_specs=(placed,) * 3,
        check_vma=False,
    )
```

```python
import functools
import math

import jax
import jax.numpy as jnp
from jax import lax
from jax.experimental import pallas as pl
from jax.experimental.pallas import tpu as pltpu
from jax.sharding import Mesh
from jax.sharding import PartitionSpec as P

AXES = ("xh", "xl", "yl", "c", "yh", "zh", "zm", "zl")
ROWS = ("xh", "xl", "yl")
PLANE = ("xh", "xl", "yl", "c", "yh")
DEPTH = ("zh", "zm", "zl")
FEATURES = 32
LOG2E = 1.4426950408889634
VMEM = pltpu.CompilerParams(vmem_limit_bytes=48 * 2**20)


def split3(v):
    one = v.astype(jnp.bfloat16).astype(jnp.float32)
    rest = v - one
    two = rest.astype(jnp.bfloat16).astype(jnp.float32)
    return one, two, rest - two


def prep_kernel(points_ref, inv_ref, dir_ref, row_ref, packed_ref):
    count = points_ref.shape[1]
    square = (FEATURES, FEATURES)
    diagonal = lax.broadcasted_iota(jnp.int32, square, 0) == lax.broadcasted_iota(jnp.int32, square, 1)
    inverse = jnp.sum(jnp.where(diagonal, inv_ref[...], 0.0), axis=1, keepdims=True)
    x = (points_ref[...].astype(jnp.float32) * inverse).astype(jnp.bfloat16).astype(jnp.float32)
    parts = split3(jnp.sum(x * x, axis=0, keepdims=True))
    place = lax.broadcasted_iota(jnp.int32, (FEATURES, count), 0)

    def operand(front, squares_at, ones_at):
        tail = jnp.where((place >= ones_at) & (place < ones_at + 3), 1.0, 0.0)
        for i, part in enumerate(parts):
            tail = jnp.where(place == squares_at + i, part, tail)
        half = count // 2
        stacked = jnp.concatenate([front[:, :half], tail[:, :half], front[:, half:], tail[:, half:]], axis=0)
        return stacked.T.astype(jnp.bfloat16)

    row_ref[...] = operand(x, 0, 3)
    packed_ref[0, :256, :] = dir_ref[...].astype(jnp.bfloat16)
    packed_ref[0, 256:, :] = operand(-2.0 * x, 3, 0)


def rows_kernel(x_ref, out_ref):
    lane = lax.broadcasted_iota(jnp.int32, (1, 128), 1)
    for j in range(x_ref.shape[0]):
        v = x_ref[j].astype(jnp.float32)
        r = pltpu.roll(v, 64, 1)
        out_ref[j, :128, :] = jnp.where(lane < 64, v, r).astype(jnp.bfloat16)
        out_ref[j, 128:, :] = jnp.where(lane < 64, r, v).astype(jnp.bfloat16)


def matern(d):
    m = jnp.maximum(d, 1e-30)
    t = m * lax.rsqrt(m)
    return (((m + 0.6) + (3.0 / math.sqrt(5.0)) * t) * jnp.exp2((-math.sqrt(5.0) * LOG2E) * t)).astype(jnp.bfloat16)


def tiles_kernel(n_bundles, has_sum, tile, *refs):
    rows_ref, bundles, refs = refs[0], refs[1 : 1 + n_bundles], refs[1 + n_bundles :]
    if has_sum:
        sum_ref, refs = refs[0], refs[1:]
    out_ref, cols_ref, dirs_ref, acc_ref, ahead_ref = refs
    pieces = bundles[0].shape[0]
    total = n_bundles * pieces
    lane = lax.broadcasted_iota(jnp.int32, (1, 128), 1)
    first = jnp.where(lane < 64, 1.0, 0.0).astype(jnp.bfloat16)
    second = jnp.where(lane < 64, 0.0, 1.0).astype(jnp.bfloat16)
    for n in range(total):
        bundle = bundles[n // pieces]
        dirs_ref[n] = bundle[n % pieces, :256, :]
        both = bundle[n % pieces, 256:, :]
        cols_ref[n, :128, :] = both * first
        cols_ref[n, 128:, :] = both * second
    acc_ref[...] = sum_ref[...] if has_sum else jnp.zeros_like(acc_ref)

    per_piece = rows_ref.shape[0] // tile

    def at(k):
        return pl.ds(pl.multiple_of((k % per_piece) * tile, tile), tile)

    def distances(k, slot):
        ahead_ref[slot] = lax.dot_general(
            rows_ref[at(k), :], cols_ref[k // per_piece], (((1,), (1,)), ((), ())), preferred_element_type=jnp.float32
        )

    distances(0, 0)

    def body(turn, _):
        for s in range(2):
            k = turn * 2 + s
            distances(jnp.minimum(k + 1, total * per_piece - 1), 1 - s)
            acc_ref[at(k), :] += jnp.dot(
                matern(ahead_ref[s]), dirs_ref[k // per_piece], preferred_element_type=jnp.float32
            )
        return 0

    lax.fori_loop(0, total * per_piece // 2, body, 0)
    out_ref[...] = acc_ref[...].astype(out_ref.dtype)


def tiles(rows, bundles, so_far, last=False):
    pieces = bundles[0].shape[0]
    n = len(bundles) * pieces
    count = rows.shape[0]
    tile = count if n > 4 else count // 2
    args = (rows, *bundles) + (() if so_far is None else (so_far,))
    whole = pl.BlockSpec(memory_space=pltpu.VMEM)
    return pl.pallas_call(
        functools.partial(tiles_kernel, len(bundles), so_far is not None, tile),
        out_shape=jax.ShapeDtypeStruct((count, 128), jnp.bfloat16 if last else jnp.float32),
        in_specs=[whole] * len(args),
        out_specs=whole,
        scratch_shapes=[
            pltpu.VMEM((n, 256, 128), jnp.bfloat16),
            pltpu.VMEM((n, 256, 128), jnp.bfloat16),
            pltpu.VMEM((count, 128), jnp.float32),
            pltpu.VMEM((2, tile, 256), jnp.float32),
        ],
        compiler_params=VMEM,
        cost_estimate=pl.CostEstimate(flops=count * n * 256 * 256, bytes_accessed=0, transcendentals=0),
    )(*args)


def image_kernel(parts_ref, noise_ref, dir_ref, res_ref, image_ref, sums_ref):
    image = (5.0 / 3.0) * jnp.sum(parts_ref[...].astype(jnp.float32), axis=0) + noise_ref[0, 0] * dir_ref[...]
    image_ref[...] = image
    res = res_ref[...]
    col = lambda v: jnp.sum(v, axis=0, keepdims=True)
    sums_ref[0:1, :] = col(res * res)
    sums_ref[1:2, :] = col(dir_ref[...] * image)
    sums_ref[2:3, :] = col(res * image)
    sums_ref[3:4, :] = col(image * image)


def step_kernel(sums_ref, image_ref, sol_ref, res_ref, dir_ref, new_sol, new_res, new_dir):
    sums = jnp.sum(sums_ref[...], axis=0)
    old_norm, curvature, cross, image_sq = (sums[i : i + 1, :] for i in range(4))
    step = old_norm / curvature
    new_norm = jnp.maximum(old_norm - 2.0 * step * cross + step * step * image_sq, 0.0)
    direction = dir_ref[...]
    new_sol[...] = sol_ref[...] + step * direction
    residual = res_ref[...] - step * image_ref[...]
    new_res[...] = residual
    new_dir[...] = residual + (new_norm / old_norm) * direction


def turned(x, axis, by):
    count = lax.axis_size(axis)
    return lax.ppermute(x, axis, [(i, (i + by) % count) for i in range(count)])


def mirrored(x, axes):
    count = lax.axis_size(axes)
    return lax.ppermute(x, axes, [(i, count - 1 - i) for i in range(count)])


def from_all(x, axes):
    count = lax.axis_size(axes)
    return lax.all_to_all(jnp.broadcast_to(x[None], (count,) + x.shape), axes, 0, 0, tiled=True)


def on_device(points, inv_length, noise_var, solution, residual, direction):
    whole = pl.BlockSpec(memory_space=pltpu.VMEM)

    def after(x, done):
        return lax.optimization_barrier((x, done))[0]

    row, packed = pl.pallas_call(
        prep_kernel,
        out_shape=(
            jax.ShapeDtypeStruct((128, 128), jnp.bfloat16),
            jax.ShapeDtypeStruct((1, 384, 128), jnp.bfloat16),
        ),
        in_specs=[whole] * 3,
        out_specs=(whole,) * 2,
        compiler_params=VMEM,
    )(points.T, inv_length.reshape(1, FEATURES), direction)

    mirror = mirrored(packed, DEPTH)
    n_rows = lax.axis_size(ROWS)
    rows = pl.pallas_call(
        rows_kernel,
        out_shape=jax.ShapeDtypeStruct((n_rows, 256, 128), jnp.bfloat16),
        in_specs=[whole],
        out_specs=whole,
        compiler_params=VMEM,
    )(from_all(row, ROWS)).reshape(n_rows * 256, 128)
    def core(x):
        return turned(x, "c", 1)

    packed_here = after(packed, rows)
    so_far = tiles(rows, [packed_here, core(packed)], None)
    mirror = after(mirror, so_far)
    pair = jnp.concatenate([packed, mirror], axis=0)
    zl, yh, zm = (turned(pair, a, 1) for a in ("zl", "yh", "zm"))
    so_far = tiles(rows, [mirror, core(mirror)], so_far)

    zl, yh = after((zl, yh), so_far)
    zl_core, yh_core, zl_yh = core(zl), core(yh), turned(zl, "yh", 1)
    so_far = tiles(rows, [zl, yh], so_far)

    zm = after(zm, so_far)
    zm_core, zm_zl, zm_yh = core(zm), turned(zm, "zl", 1), turned(zm, "yh", 1)
    so_far = tiles(rows, [zl_core, yh_core, zm], so_far)

    zl_yh, zm_yh = after((zl_yh, zm_yh), so_far)
    zl_yh_core, all_three = core(zl_yh), turned(zm_yh, "zl", 1)
    so_far = tiles(rows, [zl_yh, zm_core], so_far)

    zm_zl, zm_yh = after((zm_zl, zm_yh), so_far)
    zm_zl_core, zm_yh_core = core(zm_zl), core(zm_yh)
    so_far = tiles(rows, [zm_zl, zm_yh], so_far)

    all_three = after(all_three, so_far)
    all_three_core = core(all_three)
    so_far = tiles(rows, [zl_yh_core, zm_zl_core, zm_yh_core], so_far)
    so_far = tiles(rows, [all_three, all_three_core], so_far, True)
    parts = lax.all_to_all(so_far.reshape(n_rows, 256, 128), ROWS, 0, 0, tiled=True)
    f32 = jax.ShapeDtypeStruct(direction.shape, jnp.float32)
    image, sums = pl.pallas_call(
        image_kernel,
        out_shape=(f32, jax.ShapeDtypeStruct((4, 128), jnp.float32)),
        in_specs=[whole, pl.BlockSpec(memory_space=pltpu.SMEM), whole, whole],
        out_specs=(whole, whole),
        compiler_params=VMEM,
    )(parts, noise_var.reshape(1, 1), direction, residual)
    sums = jnp.sum(from_all(sums, PLANE), axis=0)
    sums = from_all(sums, DEPTH)
    return pl.pallas_call(
        step_kernel,
        out_shape=(f32, f32, f32),
        in_specs=[whole] * 5,
        out_specs=(whole,) * 3,
        compiler_params=VMEM,
    )(sums, image, solution, residual, direction)


def solution(mesh):
    finer = Mesh(mesh.devices.reshape((2,) * 8), AXES)
    placed = P(AXES, None)
    return jax.shard_map(
        on_device,
        mesh=finer,
        in_specs=(placed, P(), P(), placed, placed, placed),
        out_specs=(placed,) * 3,
        check_vma=False,
    )
```

```python
import functools
import math

import jax
import jax.numpy as jnp
from jax import lax
from jax.experimental import pallas as pl
from jax.experimental.pallas import tpu as pltpu
from jax.sharding import Mesh
from jax.sharding import PartitionSpec as P

AXES = ("xh", "xl", "yl", "c", "yh", "zh", "zm", "zl")
ROWS = ("xh", "xl", "yl")
PLANE = ("xh", "xl", "yl", "c", "yh")
DEPTH = ("zh", "zm", "zl")
FEATURES = 32
LOG2E = 1.4426950408889634
VMEM = pltpu.CompilerParams(vmem_limit_bytes=48 * 2**20)


def split3(v):
    one = v.astype(jnp.bfloat16).astype(jnp.float32)
    rest = v - one
    two = rest.astype(jnp.bfloat16).astype(jnp.float32)
    return one, two, rest - two


def prep_kernel(points_hbm, inv_hbm, dir_hbm, row_ref, packed_ref, points_ref, inv_ref, dir_ref, done):
    pairs = ((points_hbm, points_ref), (inv_hbm, inv_ref), (dir_hbm, dir_ref))
    copies = [pltpu.make_async_copy(a, b, done.at[i]) for i, (a, b) in enumerate(pairs)]
    for copy in copies:
        copy.start()
    for copy in copies:
        copy.wait()
    count = points_ref.shape[1]
    square = (FEATURES, FEATURES)
    diagonal = lax.broadcasted_iota(jnp.int32, square, 0) == lax.broadcasted_iota(jnp.int32, square, 1)
    inverse = jnp.sum(jnp.where(diagonal, inv_ref[...], 0.0), axis=1, keepdims=True)
    x = (points_ref[...].astype(jnp.float32) * inverse).astype(jnp.bfloat16).astype(jnp.float32)
    parts = split3(jnp.sum(x * x, axis=0, keepdims=True))
    place = lax.broadcasted_iota(jnp.int32, (FEATURES, count), 0)

    def operand(front, squares_at, ones_at):
        tail = jnp.where((place >= ones_at) & (place < ones_at + 3), 1.0, 0.0)
        for i, part in enumerate(parts):
            tail = jnp.where(place == squares_at + i, part, tail)
        half = count // 2
        stacked = jnp.concatenate([front[:, :half], tail[:, :half], front[:, half:], tail[:, half:]], axis=0)
        return stacked.T.astype(jnp.bfloat16)

    row = operand(x, 0, 3)
    for j in range(row_ref.shape[0]):
        row_ref[j] = row
    packed_ref[0, :256, :] = dir_ref[...].astype(jnp.bfloat16)
    packed_ref[0, 256:, :] = operand(-2.0 * x, 3, 0)


def rows_kernel(x_ref, out_ref):
    lane = lax.broadcasted_iota(jnp.int32, (1, 128), 1)
    for j in range(x_ref.shape[0]):
        v = x_ref[j].astype(jnp.float32)
        r = pltpu.roll(v, 64, 1)
        out_ref[j, :128, :] = jnp.where(lane < 64, v, r).astype(jnp.bfloat16)
        out_ref[j, 128:, :] = jnp.where(lane < 64, r, v).astype(jnp.bfloat16)


def matern(d):
    m = jnp.maximum(d, 1e-30)
    t = m * lax.rsqrt(m)
    return (((m + 0.6) + (3.0 / math.sqrt(5.0)) * t) * jnp.exp2((-math.sqrt(5.0) * LOG2E) * t)).astype(jnp.bfloat16)


def tiles_kernel(n_bundles, has_sum, tile, *refs):
    rows_ref, bundles, refs = refs[0], refs[1 : 1 + n_bundles], refs[1 + n_bundles :]
    if has_sum:
        sum_ref, refs = refs[0], refs[1:]
    out_ref, cols_ref, dirs_ref, ahead_ref, *refs = refs
    acc_ref = refs[0] if refs else out_ref
    pieces = bundles[0].shape[0]
    total = n_bundles * pieces
    lane = lax.broadcasted_iota(jnp.int32, (1, 128), 1)
    first = jnp.where(lane < 64, 1.0, 0.0).astype(jnp.bfloat16)
    second = jnp.where(lane < 64, 0.0, 1.0).astype(jnp.bfloat16)
    for n in range(total):
        bundle = bundles[n // pieces]
        dirs_ref[n] = bundle[n % pieces, :256, :]
        both = bundle[n % pieces, 256:, :]
        cols_ref[n, :128, :] = both * first
        cols_ref[n, 128:, :] = both * second
    if not has_sum:
        acc_ref[...] = jnp.zeros_like(acc_ref)
    elif refs:
        acc_ref[...] = sum_ref[...]

    per_piece = rows_ref.shape[0] // tile

    def at(k):
        return pl.ds(pl.multiple_of((k % per_piece) * tile, tile), tile)

    def distances(k, slot):
        ahead_ref[slot] = lax.dot_general(
            rows_ref[at(k), :], cols_ref[k // per_piece], (((1,), (1,)), ((), ())), preferred_element_type=jnp.float32
        )

    distances(0, 0)

    def body(turn, _):
        for s in range(2):
            k = turn * 2 + s
            distances(jnp.minimum(k + 1, total * per_piece - 1), 1 - s)
            acc_ref[at(k), :] += jnp.dot(
                matern(ahead_ref[s]), dirs_ref[k // per_piece], preferred_element_type=jnp.float32
            )
        return 0

    lax.fori_loop(0, total * per_piece // 2, body, 0)
    if refs:
        out_ref[...] = acc_ref[...].astype(out_ref.dtype)


def tiles(rows, bundles, so_far, last=False):
    pieces = bundles[0].shape[0]
    n = len(bundles) * pieces
    count = rows.shape[0]
    tile = count if n > 4 else count // 2
    args = (rows, *bundles) + (() if so_far is None else (so_far,))
    whole = pl.BlockSpec(memory_space=pltpu.VMEM)
    return pl.pallas_call(
        functools.partial(tiles_kernel, len(bundles), so_far is not None, tile),
        out_shape=jax.ShapeDtypeStruct((count, 128), jnp.bfloat16 if last else jnp.float32),
        in_specs=[whole] * len(args),
        out_specs=whole,
        scratch_shapes=[
            pltpu.VMEM((n, 256, 128), jnp.bfloat16),
            pltpu.VMEM((n, 256, 128), jnp.bfloat16),
            pltpu.VMEM((2, tile, 256), jnp.float32),
        ]
        + [pltpu.VMEM((count, 128), jnp.float32)] * last,
        input_output_aliases={} if so_far is None or last else {len(args) - 1: 0},
        compiler_params=VMEM,
        cost_estimate=pl.CostEstimate(flops=count * n * 256 * 256, bytes_accessed=0, transcendentals=0),
    )(*args)


def image_kernel(parts_ref, noise_ref, dir_ref, res_ref, image_ref, sums_ref):
    image = (5.0 / 3.0) * jnp.sum(parts_ref[...].astype(jnp.float32), axis=0) + noise_ref[0, 0] * dir_ref[...]
    image_ref[...] = image
    res = res_ref[...]
    col = lambda v: jnp.sum(v, axis=0, keepdims=True)
    sums_ref[0:1, :] = col(res * res)
    sums_ref[1:2, :] = col(dir_ref[...] * image)
    sums_ref[2:3, :] = col(res * image)
    sums_ref[3:4, :] = col(image * image)


def step_kernel(sums_ref, image_ref, sol_ref, res_ref, dir_ref, new_sol, new_res, new_dir):
    sums = jnp.sum(sums_ref[...], axis=0)
    old_norm, curvature, cross, image_sq = (sums[i : i + 1, :] for i in range(4))
    step = old_norm / curvature
    new_norm = jnp.maximum(old_norm - 2.0 * step * cross + step * step * image_sq, 0.0)
    direction = dir_ref[...]
    new_sol[...] = sol_ref[...] + step * direction
    residual = res_ref[...] - step * image_ref[...]
    new_res[...] = residual
    new_dir[...] = residual + (new_norm / old_norm) * direction


def turned(x, axis, by):
    count = lax.axis_size(axis)
    return lax.ppermute(x, axis, [(i, (i + by) % count) for i in range(count)])


def mirrored(x, axes):
    count = lax.axis_size(axes)
    return lax.ppermute(x, axes, [(i, count - 1 - i) for i in range(count)])


def from_all(x, axes):
    count = lax.axis_size(axes)
    return lax.all_to_all(jnp.broadcast_to(x[None], (count,) + x.shape), axes, 0, 0, tiled=True)


def on_device(points, inv_length, noise_var, solution, residual, direction):
    whole = pl.BlockSpec(memory_space=pltpu.VMEM)

    def after(x, done):
        return lax.optimization_barrier((x, done))

    def core(x):
        return turned(x, "c", 1)

    n_rows = lax.axis_size(ROWS)
    anywhere = pl.BlockSpec(memory_space=pl.ANY)
    row, own = pl.pallas_call(
        prep_kernel,
        out_shape=(
            jax.ShapeDtypeStruct((n_rows, 128, 128), jnp.bfloat16),
            jax.ShapeDtypeStruct((1, 384, 128), jnp.bfloat16),
        ),
        in_specs=[anywhere] * 3,
        out_specs=(whole,) * 2,
        scratch_shapes=[
            pltpu.VMEM((FEATURES, 256), jnp.bfloat16),
            pltpu.VMEM((1, FEATURES), jnp.float32),
            pltpu.VMEM((256, 128), jnp.float32),
            pltpu.SemaphoreType.DMA((3,)),
        ],
    )(points.T, inv_length.reshape(1, FEATURES), direction)

    zm, mirror, own_core = turned(own, "zm", 1), mirrored(own, DEPTH), core(own)
    rows = pl.pallas_call(
        rows_kernel,
        out_shape=jax.ShapeDtypeStruct((n_rows, 256, 128), jnp.bfloat16),
        in_specs=[whole],
        out_specs=whole,
        compiler_params=VMEM,
    )(lax.all_to_all(row, ROWS, 0, 0, tiled=True)).reshape(n_rows * 256, 128)

    zm, rows = after(zm, rows)
    a = jnp.concatenate([own, zm], axis=0)
    zm_core, a_zl, a_yh = core(zm), turned(a, "zl", 1), turned(a, "yh", 1)
    so_far = tiles(rows, [own, own_core], None)

    mirror, so_far = after(mirror, so_far)
    mirror_zm = turned(mirror, "zm", 1)
    so_far = tiles(rows, [zm, zm_core], so_far)

    (a_zl, a_yh), so_far = after((a_zl, a_yh), so_far)
    a_zl_core, a_yh_core, a_zl_yh = core(a_zl), core(a_yh), turned(a_zl, "yh", 1)
    so_far = tiles(rows, [a_zl, a_yh], so_far)

    mirror_zm, so_far = after(mirror_zm, so_far)
    b = jnp.concatenate([mirror, mirror_zm], axis=0)
    b_core, b_zl, b_yh = core(b), turned(b, "zl", 1), turned(b, "yh", 1)
    so_far = tiles(rows, [a_zl_core, a_yh_core, b], so_far)

    a_zl_yh, so_far = after(a_zl_yh, so_far)
    a_zl_yh_core = core(a_zl_yh)
    so_far = tiles(rows, [a_zl_yh, b_core], so_far)

    (b_zl, b_yh), so_far = after((b_zl, b_yh), so_far)
    b_zl_core, b_yh_core, b_zl_yh = core(b_zl), core(b_yh), turned(b_zl, "yh", 1)
    so_far = tiles(rows, [a_zl_yh_core, b_zl, b_yh], so_far)

    b_zl_yh, so_far = after(b_zl_yh, so_far)
    b_zl_yh_core = core(b_zl_yh)
    so_far = tiles(rows, [b_zl_core, b_yh_core, b_zl_yh], so_far)
    so_far = tiles(rows, [b_zl_yh_core], so_far, True)
    parts = lax.all_to_all(so_far.reshape(n_rows, 256, 128), ROWS, 0, 0, tiled=True)
    f32 = jax.ShapeDtypeStruct(direction.shape, jnp.float32)
    image, sums = pl.pallas_call(
        image_kernel,
        out_shape=(f32, jax.ShapeDtypeStruct((4, 128), jnp.float32)),
        in_specs=[whole, pl.BlockSpec(memory_space=pltpu.SMEM), whole, whole],
        out_specs=(whole, whole),
        compiler_params=VMEM,
    )(parts, noise_var.reshape(1, 1), direction, residual)
    sums = jnp.sum(from_all(sums, PLANE), axis=0)
    sums = from_all(sums, DEPTH)
    return pl.pallas_call(
        step_kernel,
        out_shape=(f32, f32, f32),
        in_specs=[whole] * 5,
        out_specs=(whole,) * 3,
        compiler_params=VMEM,
    )(sums, image, solution, residual, direction)


def solution(mesh):
    finer = Mesh(mesh.devices.reshape((2,) * 8), AXES)
    placed = P(AXES, None)
    return jax.shard_map(
        on_device,
        mesh=finer,
        in_specs=(placed, P(), P(), placed, placed, placed),
        out_specs=(placed,) * 3,
        check_vma=False,
    )
```

```python
import functools
import math

import jax
import jax.numpy as jnp
from jax import lax
from jax.experimental import pallas as pl
from jax.experimental.pallas import tpu as pltpu
from jax.sharding import Mesh
from jax.sharding import PartitionSpec as P

AXES = ("xh", "xl", "yl", "c", "yh", "zh", "zm", "zl")
ROWS = ("xh", "xl", "yl")
PLANE = ("xh", "xl", "yl", "c", "yh")
DEPTH = ("zh", "zm", "zl")
FEATURES = 32
LOG2E = 1.4426950408889634
VMEM = pltpu.CompilerParams(vmem_limit_bytes=48 * 2**20)


def split3(v):
    one = v.astype(jnp.bfloat16).astype(jnp.float32)
    rest = v - one
    two = rest.astype(jnp.bfloat16).astype(jnp.float32)
    return one, two, rest - two


def prep_kernel(points_hbm, inv_hbm, dir_hbm, row_ref, packed_ref, points_ref, inv_ref, dir_ref, done):
    pairs = ((points_hbm, points_ref), (inv_hbm, inv_ref), (dir_hbm, dir_ref))
    copies = [pltpu.make_async_copy(a, b, done.at[i]) for i, (a, b) in enumerate(pairs)]
    for copy in copies:
        copy.start()
    for copy in copies:
        copy.wait()
    count = points_ref.shape[1]
    square = (FEATURES, FEATURES)
    diagonal = lax.broadcasted_iota(jnp.int32, square, 0) == lax.broadcasted_iota(jnp.int32, square, 1)
    inverse = jnp.sum(jnp.where(diagonal, inv_ref[...], 0.0), axis=1, keepdims=True)
    x = (points_ref[...].astype(jnp.float32) * inverse).astype(jnp.bfloat16).astype(jnp.float32)
    parts = split3(jnp.sum(x * x, axis=0, keepdims=True))
    place = lax.broadcasted_iota(jnp.int32, (FEATURES, count), 0)

    def operand(front, squares_at, ones_at):
        tail = jnp.where((place >= ones_at) & (place < ones_at + 3), 1.0, 0.0)
        for i, part in enumerate(parts):
            tail = jnp.where(place == squares_at + i, part, tail)
        half = count // 2
        stacked = jnp.concatenate([front[:, :half], tail[:, :half], front[:, half:], tail[:, half:]], axis=0)
        return stacked.T.astype(jnp.bfloat16)

    row = operand(x, 0, 3)
    for j in range(row_ref.shape[0]):
        row_ref[j] = row
    packed_ref[0, :256, :] = dir_ref[...].astype(jnp.bfloat16)
    packed_ref[0, 256:, :] = operand(-2.0 * x, 3, 0)


def rows_kernel(x_ref, out_ref):
    lane = lax.broadcasted_iota(jnp.int32, (1, 128), 1)
    for j in range(x_ref.shape[0]):
        v = x_ref[j].astype(jnp.float32)
        r = pltpu.roll(v, 64, 1)
        out_ref[j, :128, :] = jnp.where(lane < 64, v, r).astype(jnp.bfloat16)
        out_ref[j, 128:, :] = jnp.where(lane < 64, r, v).astype(jnp.bfloat16)


def matern(d):
    m = jnp.maximum(d, 1e-30)
    t = m * lax.rsqrt(m)
    return (((m + 0.6) + (3.0 / math.sqrt(5.0)) * t) * jnp.exp2((-math.sqrt(5.0) * LOG2E) * t)).astype(jnp.bfloat16)


def tiles_kernel(n_bundles, has_sum, tile, *refs):
    rows_ref, bundles, refs = refs[0], refs[1 : 1 + n_bundles], refs[1 + n_bundles :]
    if has_sum:
        sum_ref, refs = refs[0], refs[1:]
    out_ref, cols_ref, dirs_ref, ahead_ref, *refs = refs
    acc_ref = refs[0] if refs else out_ref
    pieces = bundles[0].shape[0]
    total = n_bundles * pieces
    lane = lax.broadcasted_iota(jnp.int32, (1, 128), 1)
    first = jnp.where(lane < 64, 1.0, 0.0).astype(jnp.bfloat16)
    second = jnp.where(lane < 64, 0.0, 1.0).astype(jnp.bfloat16)
    for n in range(total):
        bundle = bundles[n // pieces]
        dirs_ref[n] = bundle[n % pieces, :256, :]
        both = bundle[n % pieces, 256:, :]
        cols_ref[n, :128, :] = both * first
        cols_ref[n, 128:, :] = both * second
    if not has_sum:
        acc_ref[...] = jnp.zeros_like(acc_ref)
    elif refs:
        acc_ref[...] = sum_ref[...]

    per_piece = rows_ref.shape[0] // tile

    def at(k):
        return pl.ds(pl.multiple_of((k % per_piece) * tile, tile), tile)

    def distances(k, slot):
        ahead_ref[slot] = lax.dot_general(
            rows_ref[at(k), :], cols_ref[k // per_piece], (((1,), (1,)), ((), ())), preferred_element_type=jnp.float32
        )

    distances(0, 0)

    def body(turn, _):
        for s in range(2):
            k = turn * 2 + s
            distances(jnp.minimum(k + 1, total * per_piece - 1), 1 - s)
            acc_ref[at(k), :] += jnp.dot(
                matern(ahead_ref[s]), dirs_ref[k // per_piece], preferred_element_type=jnp.float32
            )
        return 0

    lax.fori_loop(0, total * per_piece // 2, body, 0)
    if refs:
        out_ref[...] = acc_ref[...].astype(out_ref.dtype)


def tiles(rows, bundles, so_far, last=False):
    pieces = bundles[0].shape[0]
    n = len(bundles) * pieces
    count = rows.shape[0]
    tile = count if n > 4 else count // 2
    args = (rows, *bundles) + (() if so_far is None else (so_far,))
    whole = pl.BlockSpec(memory_space=pltpu.VMEM)
    return pl.pallas_call(
        functools.partial(tiles_kernel, len(bundles), so_far is not None, tile),
        out_shape=jax.ShapeDtypeStruct((count, 128), jnp.bfloat16 if last else jnp.float32),
        in_specs=[whole] * len(args),
        out_specs=whole,
        scratch_shapes=[
            pltpu.VMEM((n, 256, 128), jnp.bfloat16),
            pltpu.VMEM((n, 256, 128), jnp.bfloat16),
            pltpu.VMEM((2, tile, 256), jnp.float32),
        ]
        + [pltpu.VMEM((count, 128), jnp.float32)] * last,
        input_output_aliases={} if so_far is None or last else {len(args) - 1: 0},
        compiler_params=VMEM,
        cost_estimate=pl.CostEstimate(flops=count * n * 256 * 256, bytes_accessed=0, transcendentals=0),
    )(*args)


def image_kernel(parts_ref, noise_ref, dir_ref, res_ref, image_ref, sums_ref):
    image = (5.0 / 3.0) * jnp.sum(parts_ref[...].astype(jnp.float32), axis=0) + noise_ref[0, 0] * dir_ref[...]
    image_ref[...] = image
    res = res_ref[...]
    col = lambda v: jnp.sum(v, axis=0, keepdims=True)
    sums_ref[0:1, :] = col(res * res)
    sums_ref[1:2, :] = col(dir_ref[...] * image)
    sums_ref[2:3, :] = col(res * image)
    sums_ref[3:4, :] = col(image * image)


def step_kernel(sums_ref, image_ref, sol_ref, res_ref, dir_ref, new_sol, new_res, new_dir):
    sums = jnp.sum(sums_ref[...], axis=0)
    old_norm, curvature, cross, image_sq = (sums[i : i + 1, :] for i in range(4))
    step = old_norm / curvature
    new_norm = jnp.maximum(old_norm - 2.0 * step * cross + step * step * image_sq, 0.0)
    direction = dir_ref[...]
    new_sol[...] = sol_ref[...] + step * direction
    residual = res_ref[...] - step * image_ref[...]
    new_res[...] = residual
    new_dir[...] = residual + (new_norm / old_norm) * direction


def turned(x, axis, by):
    count = lax.axis_size(axis)
    return lax.ppermute(x, axis, [(i, (i + by) % count) for i in range(count)])


def mirrored(x, axes):
    count = lax.axis_size(axes)
    return lax.ppermute(x, axes, [(i, count - 1 - i) for i in range(count)])


def from_all(x, axes):
    count = lax.axis_size(axes)
    return lax.all_to_all(jnp.broadcast_to(x[None], (count,) + x.shape), axes, 0, 0, tiled=True)


def on_device(points, inv_length, noise_var, solution, residual, direction):
    whole = pl.BlockSpec(memory_space=pltpu.VMEM)

    def after(x, done):
        return lax.optimization_barrier((x, done))

    def core(x):
        return turned(x, "c", 1)

    n_rows = lax.axis_size(ROWS)
    anywhere = pl.BlockSpec(memory_space=pl.ANY)
    row, own = pl.pallas_call(
        prep_kernel,
        out_shape=(
            jax.ShapeDtypeStruct((n_rows, 128, 128), jnp.bfloat16),
            jax.ShapeDtypeStruct((1, 384, 128), jnp.bfloat16),
        ),
        in_specs=[anywhere] * 3,
        out_specs=(whole,) * 2,
        scratch_shapes=[
            pltpu.VMEM((FEATURES, 256), jnp.bfloat16),
            pltpu.VMEM((1, FEATURES), jnp.float32),
            pltpu.VMEM((256, 128), jnp.float32),
            pltpu.SemaphoreType.DMA((3,)),
        ],
    )(points.T, inv_length.reshape(1, FEATURES), direction)

    zm, mirror, own_core = turned(own, "zm", 1), mirrored(own, DEPTH), core(own)
    rows = pl.pallas_call(
        rows_kernel,
        out_shape=jax.ShapeDtypeStruct((n_rows, 256, 128), jnp.bfloat16),
        in_specs=[whole],
        out_specs=whole,
        compiler_params=VMEM,
    )(lax.all_to_all(row, ROWS, 0, 0, tiled=True)).reshape(n_rows * 256, 128)

    zm, rows = after(zm, rows)
    a = jnp.concatenate([own, zm], axis=0)
    zm_core, a_zl, a_yh = core(zm), turned(a, "zl", 1), turned(a, "yh", 1)
    mirror, rows = after(mirror, rows)
    mirror_zm = turned(mirror, "zm", 1)
    so_far = tiles(rows, [own, own_core], None)

    so_far = tiles(rows, [zm, zm_core], so_far)

    (a_zl, a_yh), so_far = after((a_zl, a_yh), so_far)
    a_zl_core, a_yh_core, a_zl_yh = core(a_zl), core(a_yh), turned(a_zl, "yh", 1)
    so_far = tiles(rows, [a_zl, a_yh], so_far)

    mirror_zm, so_far = after(mirror_zm, so_far)
    b = jnp.concatenate([mirror, mirror_zm], axis=0)
    b_core, b_zl, b_yh = core(b), turned(b, "zl", 1), turned(b, "yh", 1)
    so_far = tiles(rows, [a_zl_core, a_yh_core, b], so_far)
    so_far = tiles(rows, [a_zl_yh, b_core], so_far)

    (a_zl_yh, b_zl, b_yh), so_far = after((a_zl_yh, b_zl, b_yh), so_far)
    a_zl_yh_core, b_zl_core, b_yh_core, b_zl_yh = core(a_zl_yh), core(b_zl), core(b_yh), turned(b_zl, "yh", 1)
    so_far = tiles(rows, [b_zl, b_yh], so_far)
    so_far = tiles(rows, [a_zl_yh_core, b_zl_core], so_far)

    b_zl_yh, so_far = after(b_zl_yh, so_far)
    b_zl_yh_core = core(b_zl_yh)
    so_far = tiles(rows, [b_yh_core, b_zl_yh], so_far)
    so_far = tiles(rows, [b_zl_yh_core], so_far, True)
    parts = lax.all_to_all(so_far.reshape(n_rows, 256, 128), ROWS, 0, 0, tiled=True)
    f32 = jax.ShapeDtypeStruct(direction.shape, jnp.float32)
    image, sums = pl.pallas_call(
        image_kernel,
        out_shape=(f32, jax.ShapeDtypeStruct((4, 128), jnp.float32)),
        in_specs=[whole, pl.BlockSpec(memory_space=pltpu.SMEM), whole, whole],
        out_specs=(whole, whole),
        compiler_params=VMEM,
    )(parts, noise_var.reshape(1, 1), direction, residual)
    sums = jnp.sum(from_all(sums, PLANE), axis=0)
    sums = from_all(sums, DEPTH)
    return pl.pallas_call(
        step_kernel,
        out_shape=(f32, f32, f32),
        in_specs=[whole] * 5,
        out_specs=(whole,) * 3,
        compiler_params=VMEM,
    )(sums, image, solution, residual, direction)


def solution(mesh):
    finer = Mesh(mesh.devices.reshape((2,) * 8), AXES)
    placed = P(AXES, None)
    return jax.shard_map(
        on_device,
        mesh=finer,
        in_specs=(placed, P(), P(), placed, placed, placed),
        out_specs=(placed,) * 3,
        check_vma=False,
    )
```

```python
import functools
import math

import jax
import jax.numpy as jnp
from jax import lax
from jax.experimental import pallas as pl
from jax.experimental.pallas import tpu as pltpu
from jax.sharding import Mesh
from jax.sharding import PartitionSpec as P

AXES = ("xh", "xl", "yl", "c", "yh", "zh", "zm", "zl")
ROWS = ("xh", "xl", "yl")
PLANE = ("xh", "xl", "yl", "c", "yh")
DEPTH = ("zh", "zm", "zl")
FEATURES = 32
LOG2E = 1.4426950408889634
VMEM = pltpu.CompilerParams(vmem_limit_bytes=48 * 2**20)


def split3(v):
    one = v.astype(jnp.bfloat16).astype(jnp.float32)
    rest = v - one
    two = rest.astype(jnp.bfloat16).astype(jnp.float32)
    return one, two, rest - two


def prep_kernel(points_hbm, inv_hbm, dir_hbm, row_ref, packed_ref, points_ref, inv_ref, dir_ref, done):
    pairs = ((points_hbm, points_ref), (inv_hbm, inv_ref), (dir_hbm, dir_ref))
    copies = [pltpu.make_async_copy(a, b, done.at[i]) for i, (a, b) in enumerate(pairs)]
    for copy in copies:
        copy.start()
    for copy in copies:
        copy.wait()
    count = points_ref.shape[1]
    square = (FEATURES, FEATURES)
    diagonal = lax.broadcasted_iota(jnp.int32, square, 0) == lax.broadcasted_iota(jnp.int32, square, 1)
    inverse = jnp.sum(jnp.where(diagonal, inv_ref[...], 0.0), axis=1, keepdims=True)
    x = (points_ref[...].astype(jnp.float32) * inverse).astype(jnp.bfloat16).astype(jnp.float32)
    parts = split3(jnp.sum(x * x, axis=0, keepdims=True))
    place = lax.broadcasted_iota(jnp.int32, (FEATURES, count), 0)

    def operand(front, squares_at, ones_at):
        tail = jnp.where((place >= ones_at) & (place < ones_at + 3), 1.0, 0.0)
        for i, part in enumerate(parts):
            tail = jnp.where(place == squares_at + i, part, tail)
        half = count // 2
        stacked = jnp.concatenate([front[:, :half], tail[:, :half], front[:, half:], tail[:, half:]], axis=0)
        return stacked.T.astype(jnp.bfloat16)

    row = operand(x, 0, 3)
    for j in range(row_ref.shape[0]):
        row_ref[j] = row
    packed_ref[0, :256, :] = dir_ref[...].astype(jnp.bfloat16)
    packed_ref[0, 256:, :] = operand(-2.0 * x, 3, 0)


def rows_kernel(x_ref, out_ref):
    lane = lax.broadcasted_iota(jnp.int32, (1, 128), 1)
    for j in range(x_ref.shape[0]):
        v = x_ref[j].astype(jnp.float32)
        r = pltpu.roll(v, 64, 1)
        out_ref[j, :128, :] = jnp.where(lane < 64, v, r).astype(jnp.bfloat16)
        out_ref[j, 128:, :] = jnp.where(lane < 64, r, v).astype(jnp.bfloat16)


def matern(d):
    m = jnp.maximum(d, 1e-30)
    t = m * lax.rsqrt(m)
    return (((m + 0.6) + (3.0 / math.sqrt(5.0)) * t) * jnp.exp2((-math.sqrt(5.0) * LOG2E) * t)).astype(jnp.bfloat16)


def tiles_kernel(n_bundles, has_sum, tile, *refs):
    rows_ref, bundles, refs = refs[0], refs[1 : 1 + n_bundles], refs[1 + n_bundles :]
    if has_sum:
        sum_ref, refs = refs[0], refs[1:]
    out_ref, cols_ref, dirs_ref, ahead_ref, *refs = refs
    acc_ref = refs[0] if refs else out_ref
    pieces = [(bundle, j) for bundle in bundles for j in range(bundle.shape[0])]
    total = len(pieces)
    lane = lax.broadcasted_iota(jnp.int32, (1, 128), 1)
    first = jnp.where(lane < 64, 1.0, 0.0).astype(jnp.bfloat16)
    second = jnp.where(lane < 64, 0.0, 1.0).astype(jnp.bfloat16)
    for n, (bundle, j) in enumerate(pieces):
        dirs_ref[n] = bundle[j, :256, :]
        both = bundle[j, 256:, :]
        cols_ref[n, :128, :] = both * first
        cols_ref[n, 128:, :] = both * second
    if not has_sum:
        acc_ref[...] = jnp.zeros_like(acc_ref)
    elif refs:
        acc_ref[...] = sum_ref[...]

    per_piece = rows_ref.shape[0] // tile

    def at(k):
        return pl.ds(pl.multiple_of((k % per_piece) * tile, tile), tile)

    def distances(k, slot):
        ahead_ref[slot] = lax.dot_general(
            rows_ref[at(k), :], cols_ref[k // per_piece], (((1,), (1,)), ((), ())), preferred_element_type=jnp.float32
        )

    distances(0, 0)

    def body(turn, _):
        for s in range(2):
            k = turn * 2 + s
            distances(jnp.minimum(k + 1, total * per_piece - 1), 1 - s)
            acc_ref[at(k), :] += jnp.dot(
                matern(ahead_ref[s]), dirs_ref[k // per_piece], preferred_element_type=jnp.float32
            )
        return 0

    lax.fori_loop(0, total * per_piece // 2, body, 0)
    if refs:
        out_ref[...] = acc_ref[...].astype(out_ref.dtype)


def tiles(rows, bundles, so_far, last=False):
    n = sum(bundle.shape[0] for bundle in bundles)
    count = rows.shape[0]
    tile = count if n > 4 and n % 2 == 0 else count // 2
    args = (rows, *bundles) + (() if so_far is None else (so_far,))
    whole = pl.BlockSpec(memory_space=pltpu.VMEM)
    return pl.pallas_call(
        functools.partial(tiles_kernel, len(bundles), so_far is not None, tile),
        out_shape=jax.ShapeDtypeStruct((count, 128), jnp.bfloat16 if last else jnp.float32),
        in_specs=[whole] * len(args),
        out_specs=whole,
        scratch_shapes=[
            pltpu.VMEM((n, 256, 128), jnp.bfloat16),
            pltpu.VMEM((n, 256, 128), jnp.bfloat16),
            pltpu.VMEM((2, tile, 256), jnp.float32),
        ]
        + [pltpu.VMEM((count, 128), jnp.float32)] * last,
        input_output_aliases={} if so_far is None or last else {len(args) - 1: 0},
        compiler_params=VMEM,
        cost_estimate=pl.CostEstimate(flops=count * n * 256 * 256, bytes_accessed=0, transcendentals=0),
    )(*args)


def image_kernel(parts_ref, noise_ref, dir_ref, res_ref, image_ref, sums_ref):
    image = (5.0 / 3.0) * jnp.sum(parts_ref[...].astype(jnp.float32), axis=0) + noise_ref[0, 0] * dir_ref[...]
    image_ref[...] = image
    res = res_ref[...]
    col = lambda v: jnp.sum(v, axis=0, keepdims=True)
    sums_ref[0:1, :] = col(res * res)
    sums_ref[1:2, :] = col(dir_ref[...] * image)
    sums_ref[2:3, :] = col(res * image)
    sums_ref[3:4, :] = col(image * image)


def step_kernel(sums_ref, image_ref, sol_ref, res_ref, dir_ref, new_sol, new_res, new_dir):
    sums = jnp.sum(sums_ref[...], axis=0)
    old_norm, curvature, cross, image_sq = (sums[i : i + 1, :] for i in range(4))
    step = old_norm / curvature
    new_norm = jnp.maximum(old_norm - 2.0 * step * cross + step * step * image_sq, 0.0)
    direction = dir_ref[...]
    new_sol[...] = sol_ref[...] + step * direction
    residual = res_ref[...] - step * image_ref[...]
    new_res[...] = residual
    new_dir[...] = residual + (new_norm / old_norm) * direction


def turned(x, axis, by):
    count = lax.axis_size(axis)
    return lax.ppermute(x, axis, [(i, (i + by) % count) for i in range(count)])


def mirrored(x, axes):
    count = lax.axis_size(axes)
    return lax.ppermute(x, axes, [(i, count - 1 - i) for i in range(count)])


def from_all(x, axes):
    count = lax.axis_size(axes)
    return lax.all_to_all(jnp.broadcast_to(x[None], (count,) + x.shape), axes, 0, 0, tiled=True)


def on_device(points, inv_length, noise_var, solution, residual, direction):
    whole = pl.BlockSpec(memory_space=pltpu.VMEM)

    def after(x, done):
        return lax.optimization_barrier((x, done))

    def core(x):
        return turned(x, "c", 1)

    n_rows = lax.axis_size(ROWS)
    anywhere = pl.BlockSpec(memory_space=pl.ANY)
    row, own = pl.pallas_call(
        prep_kernel,
        out_shape=(
            jax.ShapeDtypeStruct((n_rows, 128, 128), jnp.bfloat16),
            jax.ShapeDtypeStruct((1, 384, 128), jnp.bfloat16),
        ),
        in_specs=[anywhere] * 3,
        out_specs=(whole,) * 2,
        scratch_shapes=[
            pltpu.VMEM((FEATURES, 256), jnp.bfloat16),
            pltpu.VMEM((1, FEATURES), jnp.float32),
            pltpu.VMEM((256, 128), jnp.float32),
            pltpu.SemaphoreType.DMA((3,)),
        ],
    )(points.T, inv_length.reshape(1, FEATURES), direction)

    zm, mirror, own_core = turned(own, "zm", 1), mirrored(own, DEPTH), core(own)
    rows = pl.pallas_call(
        rows_kernel,
        out_shape=jax.ShapeDtypeStruct((n_rows, 256, 128), jnp.bfloat16),
        in_specs=[whole],
        out_specs=whole,
        compiler_params=VMEM,
    )(lax.all_to_all(row, ROWS, 0, 0, tiled=True)).reshape(n_rows * 256, 128)

    so_far = tiles(rows, [own, own_core], None)

    zm, so_far = after(zm, so_far)
    a = jnp.concatenate([own, zm], axis=0)
    zm_core, a_zl, a_yh = core(zm), turned(a, "zl", 1), turned(a, "yh", 1)
    mirror, so_far = after(mirror, so_far)
    mirror_zm = turned(mirror, "zm", 1)
    so_far = tiles(rows, [zm, zm_core, mirror], so_far)

    (a_zl, a_yh), so_far = after((a_zl, a_yh), so_far)
    a_zl_core, a_yh_core, a_zl_yh = core(a_zl), core(a_yh), turned(a_zl, "yh", 1)
    so_far = tiles(rows, [a_zl, a_yh], so_far)

    mirror_zm, so_far = after(mirror_zm, so_far)
    b = jnp.concatenate([mirror, mirror_zm], axis=0)
    b_core, b_zl, b_yh = core(b), turned(b, "zl", 1), turned(b, "yh", 1)
    so_far = tiles(rows, [a_zl_core, a_yh_core, mirror_zm], so_far)
    so_far = tiles(rows, [a_zl_yh, b_core], so_far)

    (a_zl_yh, b_zl, b_yh), so_far = after((a_zl_yh, b_zl, b_yh), so_far)
    a_zl_yh_core, b_zl_core, b_yh_core, b_zl_yh = core(a_zl_yh), core(b_zl), core(b_yh), turned(b_zl, "yh", 1)
    so_far = tiles(rows, [b_zl, b_yh], so_far)
    so_far = tiles(rows, [a_zl_yh_core, b_zl_core], so_far)

    b_zl_yh, so_far = after(b_zl_yh, so_far)
    b_zl_yh_core = core(b_zl_yh)
    so_far = tiles(rows, [b_yh_core, b_zl_yh], so_far)
    so_far = tiles(rows, [b_zl_yh_core], so_far, True)
    parts = lax.all_to_all(so_far.reshape(n_rows, 256, 128), ROWS, 0, 0, tiled=True)
    f32 = jax.ShapeDtypeStruct(direction.shape, jnp.float32)
    image, sums = pl.pallas_call(
        image_kernel,
        out_shape=(f32, jax.ShapeDtypeStruct((4, 128), jnp.float32)),
        in_specs=[whole, pl.BlockSpec(memory_space=pltpu.SMEM), whole, whole],
        out_specs=(whole, whole),
        compiler_params=VMEM,
    )(parts, noise_var.reshape(1, 1), direction, residual)
    sums = jnp.sum(from_all(sums, PLANE), axis=0)
    sums = from_all(sums, DEPTH)
    return pl.pallas_call(
        step_kernel,
        out_shape=(f32, f32, f32),
        in_specs=[whole] * 5,
        out_specs=(whole,) * 3,
        compiler_params=VMEM,
    )(sums, image, solution, residual, direction)


def solution(mesh):
    finer = Mesh(mesh.devices.reshape((2,) * 8), AXES)
    placed = P(AXES, None)
    return jax.shard_map(
        on_device,
        mesh=finer,
        in_specs=(placed, P(), P(), placed, placed, placed),
        out_specs=(placed,) * 3,
        check_vma=False,
    )
```

```python
import functools
import math

import jax
import jax.numpy as jnp
from jax import lax
from jax.experimental import pallas as pl
from jax.experimental.pallas import tpu as pltpu
from jax.sharding import Mesh
from jax.sharding import PartitionSpec as P

AXES = ("xh", "xl", "yl", "c", "yh", "zh", "zm", "zl")
ROWS = ("xh", "xl", "yl")
PLANE = ("xh", "xl", "yl", "c", "yh")
DEPTH = ("zh", "zm", "zl")
FEATURES = 32
LOG2E = 1.4426950408889634
VMEM = pltpu.CompilerParams(vmem_limit_bytes=48 * 2**20)


def split3(v):
    one = v.astype(jnp.bfloat16).astype(jnp.float32)
    rest = v - one
    two = rest.astype(jnp.bfloat16).astype(jnp.float32)
    return one, two, rest - two


def prep_kernel(points_hbm, inv_hbm, dir_hbm, row_ref, packed_ref, points_ref, inv_ref, dir_ref, done):
    pairs = ((points_hbm, points_ref), (inv_hbm, inv_ref), (dir_hbm, dir_ref))
    copies = [pltpu.make_async_copy(a, b, done.at[i]) for i, (a, b) in enumerate(pairs)]
    for copy in copies:
        copy.start()
    for copy in copies:
        copy.wait()
    count = points_ref.shape[1]
    square = (FEATURES, FEATURES)
    diagonal = lax.broadcasted_iota(jnp.int32, square, 0) == lax.broadcasted_iota(jnp.int32, square, 1)
    inverse = jnp.sum(jnp.where(diagonal, inv_ref[...], 0.0), axis=1, keepdims=True)
    x = (points_ref[...].astype(jnp.float32) * inverse).astype(jnp.bfloat16).astype(jnp.float32)
    parts = split3(jnp.sum(x * x, axis=0, keepdims=True))
    place = lax.broadcasted_iota(jnp.int32, (FEATURES, count), 0)

    def operand(front, squares_at, ones_at):
        tail = jnp.where((place >= ones_at) & (place < ones_at + 3), 1.0, 0.0)
        for i, part in enumerate(parts):
            tail = jnp.where(place == squares_at + i, part, tail)
        half = count // 2
        stacked = jnp.concatenate([front[:, :half], tail[:, :half], front[:, half:], tail[:, half:]], axis=0)
        return stacked.T.astype(jnp.bfloat16)

    row = operand(x, 0, 3)
    for j in range(row_ref.shape[0]):
        row_ref[j] = row
    packed_ref[0, :256, :] = dir_ref[...].astype(jnp.bfloat16)
    packed_ref[0, 256:, :] = operand(-2.0 * x, 3, 0)


def rows_kernel(x_ref, out_ref):
    lane = lax.broadcasted_iota(jnp.int32, (1, 128), 1)
    for j in range(x_ref.shape[0]):
        v = x_ref[j].astype(jnp.float32)
        r = pltpu.roll(v, 64, 1)
        out_ref[j, :128, :] = jnp.where(lane < 64, v, r).astype(jnp.bfloat16)
        out_ref[j, 128:, :] = jnp.where(lane < 64, r, v).astype(jnp.bfloat16)


def matern(d):
    m = jnp.maximum(d, 1e-30)
    t = m * lax.rsqrt(m)
    return (((m + 0.6) + (3.0 / math.sqrt(5.0)) * t) * jnp.exp2((-math.sqrt(5.0) * LOG2E) * t)).astype(jnp.bfloat16)


def tiles_kernel(n_bundles, has_sum, tile, *refs):
    rows_ref, bundles, refs = refs[0], refs[1 : 1 + n_bundles], refs[1 + n_bundles :]
    if has_sum:
        sum_ref, refs = refs[0], refs[1:]
    out_ref, cols_ref, dirs_ref, ahead_ref, *refs = refs
    acc_ref = refs[0] if refs else out_ref
    pieces = [(bundle, j) for bundle in bundles for j in range(bundle.shape[0])]
    total = len(pieces)
    lane = lax.broadcasted_iota(jnp.int32, (1, 128), 1)
    first = jnp.where(lane < 64, 1.0, 0.0).astype(jnp.bfloat16)
    second = jnp.where(lane < 64, 0.0, 1.0).astype(jnp.bfloat16)
    for n, (bundle, j) in enumerate(pieces):
        dirs_ref[n] = bundle[j, :256, :]
        both = bundle[j, 256:, :]
        cols_ref[n, :128, :] = both * first
        cols_ref[n, 128:, :] = both * second
    if not has_sum:
        acc_ref[...] = jnp.zeros_like(acc_ref)

    per_piece = rows_ref.shape[0] // tile

    def at(k):
        start = k % per_piece * tile
        return pl.ds(start if isinstance(k, int) else pl.multiple_of(start, tile), tile)

    def distances(k, slot):
        ahead_ref[slot] = lax.dot_general(
            rows_ref[at(k), :], cols_ref[k // per_piece], (((1,), (1,)), ((), ())), preferred_element_type=jnp.float32
        )

    def products(k, slot):
        return jnp.dot(matern(ahead_ref[slot]), dirs_ref[k // per_piece], preferred_element_type=jnp.float32)

    distances(0, 0)
    count = total * per_piece
    if refs:
        for k in range(count):
            if k + 1 < count:
                distances(k + 1, (k + 1) % 2)
            so_far = (sum_ref if k < per_piece else acc_ref)[at(k), :] + products(k, k % 2)
            if k + per_piece < count:
                acc_ref[at(k), :] = so_far
            else:
                out_ref[at(k), :] = so_far.astype(out_ref.dtype)
        return

    def body(turn, _):
        for s in range(2):
            k = turn * 2 + s
            distances(jnp.minimum(k + 1, count - 1), 1 - s)
            acc_ref[at(k), :] += products(k, s)
        return 0

    lax.fori_loop(0, count // 2, body, 0)


def tiles(rows, bundles, so_far, last=False):
    n = sum(bundle.shape[0] for bundle in bundles)
    count = rows.shape[0]
    tile = count if n > 3 and n % 2 == 0 else count // 2
    args = (rows, *bundles) + (() if so_far is None else (so_far,))
    whole = pl.BlockSpec(memory_space=pltpu.VMEM)
    return pl.pallas_call(
        functools.partial(tiles_kernel, len(bundles), so_far is not None, tile),
        out_shape=jax.ShapeDtypeStruct((count, 128), jnp.bfloat16 if last else jnp.float32),
        in_specs=[whole] * len(args),
        out_specs=whole,
        scratch_shapes=[
            pltpu.VMEM((n, 256, 128), jnp.bfloat16),
            pltpu.VMEM((n, 256, 128), jnp.bfloat16),
            pltpu.VMEM((2, tile, 256), jnp.float32),
        ]
        + [pltpu.VMEM((count, 128), jnp.float32)] * last,
        input_output_aliases={} if so_far is None or last else {len(args) - 1: 0},
        compiler_params=VMEM,
        cost_estimate=pl.CostEstimate(flops=count * n * 256 * 256, bytes_accessed=0, transcendentals=0),
    )(*args)


def image_kernel(parts_ref, noise_ref, dir_ref, res_ref, image_ref, sums_ref):
    image = (5.0 / 3.0) * jnp.sum(parts_ref[...].astype(jnp.float32), axis=0) + noise_ref[0, 0] * dir_ref[...]
    image_ref[...] = image
    res = res_ref[...]
    col = lambda v: jnp.sum(v, axis=0, keepdims=True)
    sums_ref[0:1, :] = col(res * res)
    sums_ref[1:2, :] = col(dir_ref[...] * image)
    sums_ref[2:3, :] = col(res * image)
    sums_ref[3:4, :] = col(image * image)


def step_kernel(sums_ref, image_ref, sol_ref, res_ref, dir_ref, new_sol, new_res, new_dir):
    sums = jnp.sum(sums_ref[...], axis=0)
    old_norm, curvature, cross, image_sq = (sums[i : i + 1, :] for i in range(4))
    step = old_norm / curvature
    new_norm = jnp.maximum(old_norm - 2.0 * step * cross + step * step * image_sq, 0.0)
    direction = dir_ref[...]
    new_sol[...] = sol_ref[...] + step * direction
    residual = res_ref[...] - step * image_ref[...]
    new_res[...] = residual
    new_dir[...] = residual + (new_norm / old_norm) * direction


def turned(x, axis, by):
    count = lax.axis_size(axis)
    return lax.ppermute(x, axis, [(i, (i + by) % count) for i in range(count)])


def mirrored(x, axes):
    count = lax.axis_size(axes)
    return lax.ppermute(x, axes, [(i, count - 1 - i) for i in range(count)])


def from_all(x, axes):
    count = lax.axis_size(axes)
    return lax.all_to_all(jnp.broadcast_to(x[None], (count,) + x.shape), axes, 0, 0, tiled=True)


def on_device(points, inv_length, noise_var, solution, residual, direction):
    whole = pl.BlockSpec(memory_space=pltpu.VMEM)

    def after(x, done):
        return lax.optimization_barrier((x, done))

    def core(x):
        return turned(x, "c", 1)

    n_rows = lax.axis_size(ROWS)
    anywhere = pl.BlockSpec(memory_space=pl.ANY)
    row, own = pl.pallas_call(
        prep_kernel,
        out_shape=(
            jax.ShapeDtypeStruct((n_rows, 128, 128), jnp.bfloat16),
            jax.ShapeDtypeStruct((1, 384, 128), jnp.bfloat16),
        ),
        in_specs=[anywhere] * 3,
        out_specs=(whole,) * 2,
        scratch_shapes=[
            pltpu.VMEM((FEATURES, 256), jnp.bfloat16),
            pltpu.VMEM((1, FEATURES), jnp.float32),
            pltpu.VMEM((256, 128), jnp.float32),
            pltpu.SemaphoreType.DMA((3,)),
        ],
    )(points.T, inv_length.reshape(1, FEATURES), direction)

    zm, mirror, own_core = turned(own, "zm", 1), mirrored(own, DEPTH), core(own)
    rows = pl.pallas_call(
        rows_kernel,
        out_shape=jax.ShapeDtypeStruct((n_rows, 256, 128), jnp.bfloat16),
        in_specs=[whole],
        out_specs=whole,
        compiler_params=VMEM,
    )(lax.all_to_all(row, ROWS, 0, 0, tiled=True)).reshape(n_rows * 256, 128)

    so_far = tiles(rows, [own, own_core], None)

    zm, so_far = after(zm, so_far)
    a = jnp.concatenate([own, zm], axis=0)
    zm_core, a_zl, a_yh = core(zm), turned(a, "zl", 1), turned(a, "yh", 1)
    mirror, so_far = after(mirror, so_far)
    mirror_zm = turned(mirror, "zm", 1)
    so_far = tiles(rows, [zm, zm_core, mirror], so_far)

    (a_zl, a_yh), so_far = after((a_zl, a_yh), so_far)
    a_zl_core, a_yh_core, a_zl_yh = core(a_zl), core(a_yh), turned(a_zl, "yh", 1)
    so_far = tiles(rows, [a_zl, a_yh], so_far)

    mirror_zm, so_far = after(mirror_zm, so_far)
    b = jnp.concatenate([mirror, mirror_zm], axis=0)
    b_core, b_zl, b_yh = core(b), turned(b, "zl", 1), turned(b, "yh", 1)
    so_far = tiles(rows, [a_zl_core, a_yh_core, mirror_zm], so_far)
    so_far = tiles(rows, [a_zl_yh, b_core], so_far)

    (a_zl_yh, b_zl, b_yh), so_far = after((a_zl_yh, b_zl, b_yh), so_far)
    a_zl_yh_core, b_zl_core, b_yh_core, b_zl_yh = core(a_zl_yh), core(b_zl), core(b_yh), turned(b_zl, "yh", 1)
    so_far = tiles(rows, [b_zl, b_yh], so_far)
    so_far = tiles(rows, [a_zl_yh_core, b_zl_core], so_far)

    b_zl_yh, so_far = after(b_zl_yh, so_far)
    b_zl_yh_core = core(b_zl_yh)
    so_far = tiles(rows, [b_yh_core, b_zl_yh], so_far)
    so_far = tiles(rows, [b_zl_yh_core], so_far, True)
    parts = lax.all_to_all(so_far.reshape(n_rows, 256, 128), ROWS, 0, 0, tiled=True)
    f32 = jax.ShapeDtypeStruct(direction.shape, jnp.float32)
    image, sums = pl.pallas_call(
        image_kernel,
        out_shape=(f32, jax.ShapeDtypeStruct((4, 128), jnp.float32)),
        in_specs=[whole, pl.BlockSpec(memory_space=pltpu.SMEM), whole, whole],
        out_specs=(whole, whole),
        compiler_params=VMEM,
    )(parts, noise_var.reshape(1, 1), direction, residual)
    sums = jnp.sum(from_all(sums, PLANE), axis=0)
    sums = from_all(sums, DEPTH)
    return pl.pallas_call(
        step_kernel,
        out_shape=(f32, f32, f32),
        in_specs=[whole] * 5,
        out_specs=(whole,) * 3,
        compiler_params=VMEM,
    )(sums, image, solution, residual, direction)


def solution(mesh):
    finer = Mesh(mesh.devices.reshape((2,) * 8), AXES)
    placed = P(AXES, None)
    return jax.shard_map(
        on_device,
        mesh=finer,
        in_specs=(placed, P(), P(), placed, placed, placed),
        out_specs=(placed,) * 3,
        check_vma=False,
    )
```

```python
import functools
import math

import jax
import jax.numpy as jnp
from jax import lax
from jax.experimental import pallas as pl
from jax.experimental.pallas import tpu as pltpu
from jax.sharding import Mesh
from jax.sharding import PartitionSpec as P

AXES = ("xh", "xl", "yl", "c", "yh", "zh", "zm", "zl")
ROWS = ("xh", "xl", "yl")
PLANE = ("xh", "xl", "yl", "c", "yh")
DEPTH = ("zh", "zm", "zl")
FEATURES = 32
LOG2E = 1.4426950408889634
VMEM = pltpu.CompilerParams(vmem_limit_bytes=48 * 2**20)


def split3(v):
    one = v.astype(jnp.bfloat16).astype(jnp.float32)
    rest = v - one
    two = rest.astype(jnp.bfloat16).astype(jnp.float32)
    return one, two, rest - two


def prep_kernel(points_hbm, inv_hbm, dir_hbm, row_ref, packed_ref, points_ref, inv_ref, dir_ref, done):
    pairs = ((points_hbm, points_ref), (inv_hbm, inv_ref), (dir_hbm, dir_ref))
    copies = [pltpu.make_async_copy(a, b, done.at[i]) for i, (a, b) in enumerate(pairs)]
    for copy in copies:
        copy.start()
    for copy in copies:
        copy.wait()
    count = points_ref.shape[1]
    square = (FEATURES, FEATURES)
    diagonal = lax.broadcasted_iota(jnp.int32, square, 0) == lax.broadcasted_iota(jnp.int32, square, 1)
    inverse = jnp.sum(jnp.where(diagonal, inv_ref[...], 0.0), axis=1, keepdims=True)
    x = (points_ref[...].astype(jnp.float32) * inverse).astype(jnp.bfloat16).astype(jnp.float32)
    parts = split3(jnp.sum(x * x, axis=0, keepdims=True))
    place = lax.broadcasted_iota(jnp.int32, (FEATURES, count), 0)

    def operand(front, squares_at, ones_at):
        tail = jnp.where((place >= ones_at) & (place < ones_at + 3), 1.0, 0.0)
        for i, part in enumerate(parts):
            tail = jnp.where(place == squares_at + i, part, tail)
        half = count // 2
        stacked = jnp.concatenate([front[:, :half], tail[:, :half], front[:, half:], tail[:, half:]], axis=0)
        return stacked.T.astype(jnp.bfloat16)

    row = operand(x, 0, 3)
    for j in range(row_ref.shape[0]):
        row_ref[j] = row
    packed_ref[0, :256, :] = dir_ref[...].astype(jnp.bfloat16)
    packed_ref[0, 256:, :] = operand(-2.0 * x, 3, 0)


def rows_kernel(x_ref, out_ref):
    lane = lax.broadcasted_iota(jnp.int32, (1, 128), 1)
    for j in range(x_ref.shape[0]):
        v = x_ref[j].astype(jnp.float32)
        r = pltpu.roll(v, 64, 1)
        out_ref[j, :128, :] = jnp.where(lane < 64, v, r).astype(jnp.bfloat16)
        out_ref[j, 128:, :] = jnp.where(lane < 64, r, v).astype(jnp.bfloat16)


def matern(d):
    m = jnp.maximum(d, 1e-30)
    t = m * lax.rsqrt(m)
    return (((m + 0.6) + (3.0 / math.sqrt(5.0)) * t) * jnp.exp2((-math.sqrt(5.0) * LOG2E) * t)).astype(jnp.bfloat16)


def tiles_kernel(n_bundles, has_sum, tile, *refs):
    rows_ref, bundles, refs = refs[0], refs[1 : 1 + n_bundles], refs[1 + n_bundles :]
    if has_sum:
        sum_ref, refs = refs[0], refs[1:]
    out_ref, cols_ref, dirs_ref, ahead_ref, *refs = refs
    acc_ref = refs[0] if refs else out_ref
    pieces = [(bundle, j) for bundle in bundles for j in range(bundle.shape[0])]
    total = len(pieces)
    lane = lax.broadcasted_iota(jnp.int32, (1, 128), 1)
    first = jnp.where(lane < 64, 1.0, 0.0).astype(jnp.bfloat16)
    second = jnp.where(lane < 64, 0.0, 1.0).astype(jnp.bfloat16)
    for n, (bundle, j) in enumerate(pieces):
        dirs_ref[n] = bundle[j, :256, :]
        both = bundle[j, 256:, :]
        cols_ref[n, :128, :] = both * first
        cols_ref[n, 128:, :] = both * second
    if not has_sum:
        acc_ref[...] = jnp.zeros_like(acc_ref)

    per_piece = rows_ref.shape[0] // tile

    def at(k):
        start = k % per_piece * tile
        return pl.ds(start if isinstance(k, int) else pl.multiple_of(start, tile), tile)

    def distances(k, slot):
        ahead_ref[slot] = lax.dot_general(
            rows_ref[at(k), :], cols_ref[k // per_piece], (((1,), (1,)), ((), ())), preferred_element_type=jnp.float32
        )

    def products(k, slot):
        return jnp.dot(matern(ahead_ref[slot]), dirs_ref[k // per_piece], preferred_element_type=jnp.float32)

    distances(0, 0)
    count = total * per_piece
    if refs:
        for k in range(count):
            if k + 1 < count:
                distances(k + 1, (k + 1) % 2)
            so_far = (sum_ref if k < per_piece else acc_ref)[at(k), :] + products(k, k % 2)
            if k + per_piece < count:
                acc_ref[at(k), :] = so_far
            else:
                out_ref[at(k), :] = so_far.astype(out_ref.dtype)
        return

    if count == 4:
        for k in range(count):
            if k + 1 < count:
                distances(k + 1, (k + 1) % 2)
            acc_ref[at(k), :] += products(k, k % 2)
        return

    def body(turn, _):
        for s in range(2):
            k = turn * 2 + s
            distances(jnp.minimum(k + 1, count - 1), 1 - s)
            acc_ref[at(k), :] += products(k, s)
        return 0

    lax.fori_loop(0, count // 2, body, 0)


def tiles(rows, bundles, so_far, last=False):
    n = sum(bundle.shape[0] for bundle in bundles)
    count = rows.shape[0]
    tile = count if n > 3 and n % 2 == 0 else count // 2
    args = (rows, *bundles) + (() if so_far is None else (so_far,))
    whole = pl.BlockSpec(memory_space=pltpu.VMEM)
    return pl.pallas_call(
        functools.partial(tiles_kernel, len(bundles), so_far is not None, tile),
        out_shape=jax.ShapeDtypeStruct((count, 128), jnp.bfloat16 if last else jnp.float32),
        in_specs=[whole] * len(args),
        out_specs=whole,
        scratch_shapes=[
            pltpu.VMEM((n, 256, 128), jnp.bfloat16),
            pltpu.VMEM((n, 256, 128), jnp.bfloat16),
            pltpu.VMEM((2, tile, 256), jnp.float32),
        ]
        + [pltpu.VMEM((count, 128), jnp.float32)] * last,
        input_output_aliases={} if so_far is None or last else {len(args) - 1: 0},
        compiler_params=VMEM,
        cost_estimate=pl.CostEstimate(flops=count * n * 256 * 256, bytes_accessed=0, transcendentals=0),
    )(*args)


def image_kernel(parts_ref, noise_ref, dir_ref, res_ref, image_ref, sums_ref):
    image = (5.0 / 3.0) * jnp.sum(parts_ref[...].astype(jnp.float32), axis=0) + noise_ref[0, 0] * dir_ref[...]
    image_ref[...] = image
    res = res_ref[...]
    col = lambda v: jnp.sum(v, axis=0, keepdims=True)
    sums_ref[0:1, :] = col(res * res)
    sums_ref[1:2, :] = col(dir_ref[...] * image)
    sums_ref[2:3, :] = col(res * image)
    sums_ref[3:4, :] = col(image * image)


def step_kernel(sums_ref, image_ref, sol_ref, res_ref, dir_ref, new_sol, new_res, new_dir):
    sums = jnp.sum(sums_ref[...], axis=0)
    old_norm, curvature, cross, image_sq = (sums[i : i + 1, :] for i in range(4))
    step = old_norm / curvature
    new_norm = jnp.maximum(old_norm - 2.0 * step * cross + step * step * image_sq, 0.0)
    direction = dir_ref[...]
    new_sol[...] = sol_ref[...] + step * direction
    residual = res_ref[...] - step * image_ref[...]
    new_res[...] = residual
    new_dir[...] = residual + (new_norm / old_norm) * direction


def turned(x, axis, by):
    count = lax.axis_size(axis)
    return lax.ppermute(x, axis, [(i, (i + by) % count) for i in range(count)])


def mirrored(x, axes):
    count = lax.axis_size(axes)
    return lax.ppermute(x, axes, [(i, count - 1 - i) for i in range(count)])


def from_all(x, axes):
    count = lax.axis_size(axes)
    return lax.all_to_all(jnp.broadcast_to(x[None], (count,) + x.shape), axes, 0, 0, tiled=True)


def on_device(points, inv_length, noise_var, solution, residual, direction):
    whole = pl.BlockSpec(memory_space=pltpu.VMEM)

    def after(x, done):
        return lax.optimization_barrier((x, done))

    def core(x):
        return turned(x, "c", 1)

    n_rows = lax.axis_size(ROWS)
    anywhere = pl.BlockSpec(memory_space=pl.ANY)
    row, own = pl.pallas_call(
        prep_kernel,
        out_shape=(
            jax.ShapeDtypeStruct((n_rows, 128, 128), jnp.bfloat16),
            jax.ShapeDtypeStruct((1, 384, 128), jnp.bfloat16),
        ),
        in_specs=[anywhere] * 3,
        out_specs=(whole,) * 2,
        scratch_shapes=[
            pltpu.VMEM((FEATURES, 256), jnp.bfloat16),
            pltpu.VMEM((1, FEATURES), jnp.float32),
            pltpu.VMEM((256, 128), jnp.float32),
            pltpu.SemaphoreType.DMA((3,)),
        ],
    )(points.T, inv_length.reshape(1, FEATURES), direction)

    zm, mirror, own_core = turned(own, "zm", 1), mirrored(own, DEPTH), core(own)
    rows = pl.pallas_call(
        rows_kernel,
        out_shape=jax.ShapeDtypeStruct((n_rows, 256, 128), jnp.bfloat16),
        in_specs=[whole],
        out_specs=whole,
        compiler_params=VMEM,
    )(lax.all_to_all(row, ROWS, 0, 0, tiled=True)).reshape(n_rows * 256, 128)

    so_far = tiles(rows, [own, own_core], None)

    zm, so_far = after(zm, so_far)
    a = jnp.concatenate([own, zm], axis=0)
    zm_core, a_zl, a_yh = core(zm), turned(a, "zl", 1), turned(a, "yh", 1)
    mirror, so_far = after(mirror, so_far)
    mirror_zm = turned(mirror, "zm", 1)
    so_far = tiles(rows, [zm, zm_core, mirror], so_far)

    (a_zl, a_yh), so_far = after((a_zl, a_yh), so_far)
    a_zl_core, a_yh_core, a_zl_yh = core(a_zl), core(a_yh), turned(a_zl, "yh", 1)
    so_far = tiles(rows, [a_zl, a_yh], so_far)

    mirror_zm, so_far = after(mirror_zm, so_far)
    b = jnp.concatenate([mirror, mirror_zm], axis=0)
    b_core, b_zl, b_yh = core(b), turned(b, "zl", 1), turned(b, "yh", 1)
    so_far = tiles(rows, [a_zl_core, a_yh_core, mirror_zm], so_far)
    so_far = tiles(rows, [a_zl_yh, b_core], so_far)

    (a_zl_yh, b_zl, b_yh), so_far = after((a_zl_yh, b_zl, b_yh), so_far)
    a_zl_yh_core, b_zl_core, b_yh_core, b_zl_yh = core(a_zl_yh), core(b_zl), core(b_yh), turned(b_zl, "yh", 1)
    so_far = tiles(rows, [b_zl, b_yh], so_far)
    so_far = tiles(rows, [a_zl_yh_core, b_zl_core], so_far)

    b_zl_yh, so_far = after(b_zl_yh, so_far)
    b_zl_yh_core = core(b_zl_yh)
    so_far = tiles(rows, [b_yh_core, b_zl_yh], so_far)
    so_far = tiles(rows, [b_zl_yh_core], so_far, True)
    parts = lax.all_to_all(so_far.reshape(n_rows, 256, 128), ROWS, 0, 0, tiled=True)
    f32 = jax.ShapeDtypeStruct(direction.shape, jnp.float32)
    image, sums = pl.pallas_call(
        image_kernel,
        out_shape=(f32, jax.ShapeDtypeStruct((4, 128), jnp.float32)),
        in_specs=[whole, pl.BlockSpec(memory_space=pltpu.SMEM), whole, whole],
        out_specs=(whole, whole),
        compiler_params=VMEM,
    )(parts, noise_var.reshape(1, 1), direction, residual)
    sums = jnp.sum(from_all(sums, PLANE), axis=0)
    sums = from_all(sums, DEPTH)
    return pl.pallas_call(
        step_kernel,
        out_shape=(f32, f32, f32),
        in_specs=[whole] * 5,
        out_specs=(whole,) * 3,
        compiler_params=VMEM,
    )(sums, image, solution, residual, direction)


def solution(mesh):
    finer = Mesh(mesh.devices.reshape((2,) * 8), AXES)
    placed = P(AXES, None)
    return jax.shard_map(
        on_device,
        mesh=finer,
        in_specs=(placed, P(), P(), placed, placed, placed),
        out_specs=(placed,) * 3,
        check_vma=False,
    )
```

```python
import functools
import math

import jax
import jax.numpy as jnp
from jax import lax
from jax.experimental import pallas as pl
from jax.experimental.pallas import tpu as pltpu
from jax.sharding import Mesh
from jax.sharding import PartitionSpec as P

AXES = ("xh", "xl", "yl", "c", "yh", "zh", "zm", "zl")
ROWS = ("xh", "xl", "yl")
PLANE = ("xh", "xl", "yl", "c", "yh")
DEPTH = ("zh", "zm", "zl")
FEATURES = 32
LOG2E = 1.4426950408889634
VMEM = pltpu.CompilerParams(vmem_limit_bytes=48 * 2**20)


def split3(v):
    one = v.astype(jnp.bfloat16).astype(jnp.float32)
    rest = v - one
    two = rest.astype(jnp.bfloat16).astype(jnp.float32)
    return one, two, rest - two


def prep_kernel(points_hbm, inv_hbm, dir_hbm, row_ref, packed_ref, points_ref, inv_ref, dir_ref, done):
    pairs = ((points_hbm, points_ref), (inv_hbm, inv_ref), (dir_hbm, dir_ref))
    copies = [pltpu.make_async_copy(a, b, done.at[i]) for i, (a, b) in enumerate(pairs)]
    for copy in copies:
        copy.start()
    for copy in copies:
        copy.wait()
    count = points_ref.shape[1]
    square = (FEATURES, FEATURES)
    diagonal = lax.broadcasted_iota(jnp.int32, square, 0) == lax.broadcasted_iota(jnp.int32, square, 1)
    inverse = jnp.sum(jnp.where(diagonal, inv_ref[...], 0.0), axis=1, keepdims=True)
    x = (points_ref[...].astype(jnp.float32) * inverse).astype(jnp.bfloat16).astype(jnp.float32)
    parts = split3(jnp.sum(x * x, axis=0, keepdims=True))
    place = lax.broadcasted_iota(jnp.int32, (FEATURES, count), 0)

    def operand(front, squares_at, ones_at):
        tail = jnp.where((place >= ones_at) & (place < ones_at + 3), 1.0, 0.0)
        for i, part in enumerate(parts):
            tail = jnp.where(place == squares_at + i, part, tail)
        half = count // 2
        stacked = jnp.concatenate([front[:, :half], tail[:, :half], front[:, half:], tail[:, half:]], axis=0)
        return stacked.T.astype(jnp.bfloat16)

    row = operand(x, 0, 3)
    for j in range(row_ref.shape[0]):
        row_ref[j] = row
    packed_ref[0, :256, :] = dir_ref[...].astype(jnp.bfloat16)
    packed_ref[0, 256:, :] = operand(-2.0 * x, 3, 0)


def rows_kernel(x_ref, out_ref):
    lane = lax.broadcasted_iota(jnp.int32, (1, 128), 1)
    for j in range(x_ref.shape[0]):
        v = x_ref[j].astype(jnp.float32)
        r = pltpu.roll(v, 64, 1)
        out_ref[j, :128, :] = jnp.where(lane < 64, v, r).astype(jnp.bfloat16)
        out_ref[j, 128:, :] = jnp.where(lane < 64, r, v).astype(jnp.bfloat16)


def matern(d):
    m = jnp.maximum(d, 1e-30)
    t = m * lax.rsqrt(m)
    return (((m + 0.6) + (3.0 / math.sqrt(5.0)) * t) * jnp.exp2((-math.sqrt(5.0) * LOG2E) * t)).astype(jnp.bfloat16)


def tiles_kernel(n_bundles, has_sum, tile, *refs):
    rows_ref, bundles, refs = refs[0], refs[1 : 1 + n_bundles], refs[1 + n_bundles :]
    if has_sum:
        sum_ref, refs = refs[0], refs[1:]
    out_ref, cols_ref, dirs_ref, ahead_ref, *refs = refs
    acc_ref = refs[0] if refs else out_ref
    pieces = [(bundle, j) for bundle in bundles for j in range(bundle.shape[0])]
    total = len(pieces)
    lane = lax.broadcasted_iota(jnp.int32, (1, 128), 1)
    first = jnp.where(lane < 64, 1.0, 0.0).astype(jnp.bfloat16)
    second = jnp.where(lane < 64, 0.0, 1.0).astype(jnp.bfloat16)
    for n, (bundle, j) in enumerate(pieces):
        dirs_ref[n] = bundle[j, :256, :]
        both = bundle[j, 256:, :]
        cols_ref[n, :128, :] = both * first
        cols_ref[n, 128:, :] = both * second
    if not has_sum:
        acc_ref[...] = jnp.zeros_like(acc_ref)

    per_piece = rows_ref.shape[0] // tile

    def at(k):
        start = k % per_piece * tile
        return pl.ds(start if isinstance(k, int) else pl.multiple_of(start, tile), tile)

    def distances(k, slot):
        ahead_ref[slot] = lax.dot_general(
            rows_ref[at(k), :], cols_ref[k // per_piece], (((1,), (1,)), ((), ())), preferred_element_type=jnp.float32
        )

    def products(k, slot):
        return jnp.dot(matern(ahead_ref[slot]), dirs_ref[k // per_piece], preferred_element_type=jnp.float32)

    distances(0, 0)
    count = total * per_piece
    if refs:
        for k in range(count):
            if k + 1 < count:
                distances(k + 1, (k + 1) % 2)
            so_far = (sum_ref if k < per_piece else acc_ref)[at(k), :] + products(k, k % 2)
            if k + per_piece < count:
                acc_ref[at(k), :] = so_far
            else:
                out_ref[at(k), :] = so_far.astype(out_ref.dtype)
        return

    if count in (4, 5, 6):
        for k in range(count):
            if k + 1 < count:
                distances(k + 1, (k + 1) % 2)
            acc_ref[at(k), :] += products(k, k % 2)
        return

    def body(turn, _):
        for s in range(2):
            k = turn * 2 + s
            distances(jnp.minimum(k + 1, count - 1), 1 - s)
            acc_ref[at(k), :] += products(k, s)
        return 0

    lax.fori_loop(0, count // 2, body, 0)


def tiles(rows, bundles, so_far, last=False):
    n = sum(bundle.shape[0] for bundle in bundles)
    count = rows.shape[0]
    tile = count if n > 3 else count // 2
    args = (rows, *bundles) + (() if so_far is None else (so_far,))
    whole = pl.BlockSpec(memory_space=pltpu.VMEM)
    return pl.pallas_call(
        functools.partial(tiles_kernel, len(bundles), so_far is not None, tile),
        out_shape=jax.ShapeDtypeStruct((count, 128), jnp.bfloat16 if last else jnp.float32),
        in_specs=[whole] * len(args),
        out_specs=whole,
        scratch_shapes=[
            pltpu.VMEM((n, 256, 128), jnp.bfloat16),
            pltpu.VMEM((n, 256, 128), jnp.bfloat16),
            pltpu.VMEM((2, tile, 256), jnp.float32),
        ]
        + [pltpu.VMEM((count, 128), jnp.float32)] * last,
        input_output_aliases={} if so_far is None or last else {len(args) - 1: 0},
        compiler_params=VMEM,
        cost_estimate=pl.CostEstimate(flops=count * n * 256 * 256, bytes_accessed=0, transcendentals=0),
    )(*args)


def image_kernel(parts_ref, noise_ref, dir_ref, res_ref, image_ref, sums_ref):
    image = (5.0 / 3.0) * jnp.sum(parts_ref[...].astype(jnp.float32), axis=0) + noise_ref[0, 0] * dir_ref[...]
    image_ref[...] = image
    res = res_ref[...]
    col = lambda v: jnp.sum(v, axis=0, keepdims=True)
    sums_ref[0:1, :] = col(res * res)
    sums_ref[1:2, :] = col(dir_ref[...] * image)
    sums_ref[2:3, :] = col(res * image)
    sums_ref[3:4, :] = col(image * image)


def step_kernel(sums_ref, image_ref, sol_ref, res_ref, dir_ref, new_sol, new_res, new_dir):
    sums = jnp.sum(sums_ref[...], axis=0)
    old_norm, curvature, cross, image_sq = (sums[i : i + 1, :] for i in range(4))
    step = old_norm / curvature
    new_norm = jnp.maximum(old_norm - 2.0 * step * cross + step * step * image_sq, 0.0)
    direction = dir_ref[...]
    new_sol[...] = sol_ref[...] + step * direction
    residual = res_ref[...] - step * image_ref[...]
    new_res[...] = residual
    new_dir[...] = residual + (new_norm / old_norm) * direction


def turned(x, axis, by):
    count = lax.axis_size(axis)
    return lax.ppermute(x, axis, [(i, (i + by) % count) for i in range(count)])


def mirrored(x, axes):
    count = lax.axis_size(axes)
    return lax.ppermute(x, axes, [(i, count - 1 - i) for i in range(count)])


def from_all(x, axes):
    count = lax.axis_size(axes)
    return lax.all_to_all(jnp.broadcast_to(x[None], (count,) + x.shape), axes, 0, 0, tiled=True)


def on_device(points, inv_length, noise_var, solution, residual, direction):
    whole = pl.BlockSpec(memory_space=pltpu.VMEM)

    def after(x, done):
        return lax.optimization_barrier((x, done))

    def core(x):
        return turned(x, "c", 1)

    n_rows = lax.axis_size(ROWS)
    anywhere = pl.BlockSpec(memory_space=pl.ANY)
    row, own = pl.pallas_call(
        prep_kernel,
        out_shape=(
            jax.ShapeDtypeStruct((n_rows, 128, 128), jnp.bfloat16),
            jax.ShapeDtypeStruct((1, 384, 128), jnp.bfloat16),
        ),
        in_specs=[anywhere] * 3,
        out_specs=(whole,) * 2,
        scratch_shapes=[
            pltpu.VMEM((FEATURES, 256), jnp.bfloat16),
            pltpu.VMEM((1, FEATURES), jnp.float32),
            pltpu.VMEM((256, 128), jnp.float32),
            pltpu.SemaphoreType.DMA((3,)),
        ],
    )(points.T, inv_length.reshape(1, FEATURES), direction)

    zm, mirror, own_core = turned(own, "zm", 1), mirrored(own, DEPTH), core(own)
    rows = pl.pallas_call(
        rows_kernel,
        out_shape=jax.ShapeDtypeStruct((n_rows, 256, 128), jnp.bfloat16),
        in_specs=[whole],
        out_specs=whole,
        compiler_params=VMEM,
    )(lax.all_to_all(row, ROWS, 0, 0, tiled=True)).reshape(n_rows * 256, 128)

    so_far = tiles(rows, [own, own_core], None)

    zm, so_far = after(zm, so_far)
    a = jnp.concatenate([own, zm], axis=0)
    zm_core, a_zl, a_yh = core(zm), turned(a, "zl", 1), turned(a, "yh", 1)
    mirror, so_far = after(mirror, so_far)
    mirror_zm = turned(mirror, "zm", 1)
    so_far = tiles(rows, [zm, zm_core, mirror], so_far)

    (a_zl, a_yh), so_far = after((a_zl, a_yh), so_far)
    a_zl_core, a_yh_core, a_zl_yh = core(a_zl), core(a_yh), turned(a_zl, "yh", 1)
    so_far = tiles(rows, [a_zl, a_yh], so_far)

    mirror_zm, so_far = after(mirror_zm, so_far)
    b = jnp.concatenate([mirror, mirror_zm], axis=0)
    b_core, b_zl, b_yh = core(b), turned(b, "zl", 1), turned(b, "yh", 1)
    so_far = tiles(rows, [a_zl_core, a_yh_core, mirror_zm], so_far)
    so_far = tiles(rows, [a_zl_yh, b_core], so_far)

    (a_zl_yh, b_zl, b_yh), so_far = after((a_zl_yh, b_zl, b_yh), so_far)
    a_zl_yh_core, b_zl_core, b_yh_core, b_zl_yh = core(a_zl_yh), core(b_zl), core(b_yh), turned(b_zl, "yh", 1)
    so_far = tiles(rows, [b_zl, b_yh], so_far)
    so_far = tiles(rows, [a_zl_yh_core, b_zl_core], so_far)

    b_zl_yh, so_far = after(b_zl_yh, so_far)
    b_zl_yh_core = core(b_zl_yh)
    so_far = tiles(rows, [b_yh_core, b_zl_yh], so_far)
    so_far = tiles(rows, [b_zl_yh_core], so_far, True)
    parts = lax.all_to_all(so_far.reshape(n_rows, 256, 128), ROWS, 0, 0, tiled=True)
    f32 = jax.ShapeDtypeStruct(direction.shape, jnp.float32)
    image, sums = pl.pallas_call(
        image_kernel,
        out_shape=(f32, jax.ShapeDtypeStruct((4, 128), jnp.float32)),
        in_specs=[whole, pl.BlockSpec(memory_space=pltpu.SMEM), whole, whole],
        out_specs=(whole, whole),
        compiler_params=VMEM,
    )(parts, noise_var.reshape(1, 1), direction, residual)
    sums = jnp.sum(from_all(sums, PLANE), axis=0)
    sums = from_all(sums, DEPTH)
    return pl.pallas_call(
        step_kernel,
        out_shape=(f32, f32, f32),
        in_specs=[whole] * 5,
        out_specs=(whole,) * 3,
        compiler_params=VMEM,
    )(sums, image, solution, residual, direction)


def solution(mesh):
    finer = Mesh(mesh.devices.reshape((2,) * 8), AXES)
    placed = P(AXES, None)
    return jax.shard_map(
        on_device,
        mesh=finer,
        in_specs=(placed, P(), P(), placed, placed, placed),
        out_specs=(placed,) * 3,
        check_vma=False,
    )
```
